32 devices in a mesh: grp: 2 (over x), gx: 16 (over z, y, core).
Axes of the slice: x: 2, y: 2, z: 4, core: 2. Of those that a mesh axis runs over, the one named last changes fastest.
Arguments:
- layer_input: bfloat16 [512, 9216], P(('grp', 'gx')), parts along dimension 0, may hold values from -6 to 6
- norm_gain: float32 [9216], replicated, may hold values from 0.1 to 1.9
- w_query: bfloat16 [9216, 6144], P(None, 'gx'), may hold values from -2 to 2
- w_keyval: bfloat16 [9216, 512], P(None, 'gx'), may hold values from -0.0625 to 0.0625
- w_out: bfloat16 [6144, 9216], P('gx'), may hold values from -0.078125 to 0.078125
- w_gate: bfloat16 [9216, 9216], P(None, 'gx'), may hold values from -0.0625 to 0.0625
- w_up: bfloat16 [9216, 9216], P(None, 'gx'), may hold values from -0.0625 to 0.0625
- w_down: bfloat16 [9216, 9216], P('gx'), may hold values from -0.0625 to 0.0625
- cache_keys: bfloat16 [512, 256, 256], P(('grp', 'gx')), parts along dimension 0, may hold values from -6 to 6
- cache_values: bfloat16 [512, 256, 256], P(('grp', 'gx')), parts along dimension 0, may hold values from -6 to 6
- lengths: int32 [512], P(('grp', 'gx')), parts along dimension 0, may hold values from 2 to 256, as said below
Outputs:
- layer_output: bfloat16 [512, 9216], P(('grp', 'gx')), parts along dimension 0
The draws below stay inside these ranges and needn't reach their ends.
There are 2 independent parts, one for each index of `grp`. The reference program is written for one: setup_inputs(seed, part) draws one part's arguments, and reference() takes and returns one part's arrays. A program takes and returns all parts, laid end to end along the dimension named above; an argument that names none is the same for every part. Nothing has to cross between parts.
Inputs may be any that keep to these rules, and one draw needn't show every extreme that they name: `lengths`: each row's count of cached tokens; some row of every replica holds all 256.
All inputs are finite; a program needn't handle non-finite values.
Results may differ from the reference program's by a relative error of at most 0.0057.
Values may be sent and summed in bfloat16 or wider, within the bound.
A program may use at most 192 MiB of HBM per device.

```python
import math
import jax
import jax.numpy as jnp
from jax import lax

D = 9216
H = 24
HD = 256
FF = 9216
L = 256
ROW_DEV = 16
ROWS = 256


def draw_layer_input(key, part):
    key = jax.random.fold_in(key, 23)
    noise_key = jax.random.fold_in(key, 0)
    values = jnp.clip(jax.random.normal(noise_key, (ROWS, D), jnp.float32), -6.0, 6.0)
    return values.astype(jnp.bfloat16)


def draw_w_query(key, part):
    key = jax.random.fold_in(key, 31)
    normal_key = jax.random.fold_in(key, 0)
    values = jnp.clip(jax.random.normal(normal_key, (D, H * HD), jnp.float32), -4.0, 4.0) / math.sqrt(D)
    return values.astype(jnp.bfloat16)


def draw_cache_keys(key, part):
    key = jax.random.fold_in(key, 47)
    values = jnp.clip(jax.random.normal(key, (ROWS, L, HD), jnp.float32), -6.0, 6.0)
    return values.astype(jnp.bfloat16)


def draw_lengths(key, part):
    key = jax.random.fold_in(key, 11)
    first_key, second_key, third_key = jax.random.split(key, 3)
    devices_count = ROWS // ROW_DEV
    ceilings = jax.random.randint(first_key, (devices_count, 1), max(L // 8, 2), L + 1)
    uniform_bits = jax.random.randint(second_key, (devices_count, ROW_DEV), 0, 1 << 20)
    drawn = (2 + uniform_bits % (ceilings - 1)).reshape(ROWS)
    chosen = jax.random.randint(third_key, (), 0, ROWS)
    drawn = jnp.where(jnp.arange(ROWS, dtype=jnp.int32) == chosen, L, drawn)
    return drawn.astype(jnp.int32)


def steps_of(own_key, extent, cuts, smallest, largest):
    loudness, own = 1.0, jax.random.fold_in(own_key, 6)
    for position, parts in cuts:
        heights = jnp.exp(jax.random.uniform(jax.random.fold_in(own, position), (parts,), jnp.float32, smallest / len(cuts), largest / len(cuts)))
        loudness = loudness * jnp.repeat(heights, extent[position] // parts).reshape([-1 if axis == position else 1 for axis in range(len(extent))])
    return loudness


def scatter_about(key, shape, scale, most, pieces=(), kind=jnp.bfloat16):
    values = jax.random.normal(key, shape, jnp.float32) * scale
    if len(pieces) > 0:
        values = steps_of(key, shape, pieces, -0.22, 0.18) * values
    return jnp.clip(values, min=-most, max=most).astype(kind)


def setup_inputs(seed: int = 0, part: int = 0) -> dict:
    key_of = jax.random.split(jax.random.key(seed), 12)
    part_keys = jax.random.split(jax.random.fold_in(key_of[11], part), 12)
    layer_input = draw_layer_input(jax.random.fold_in(jax.random.fold_in(key_of[11], part), 71), part)
    norm_gain = jnp.clip(1.0 + 0.18 * jax.random.normal(key_of[1], (D,), jnp.float32), 0.1, 1.9)
    w_query = draw_w_query(jax.random.fold_in(key_of[11], 71), part)
    w_keyval = scatter_about(key_of[3], (D, 2 * HD), D ** -0.5, 0.0625, ((1, 16),))
    w_out = scatter_about(key_of[4], (H * HD, D), (H * HD) ** -0.5, 0.078125, ((0, 16),))
    w_gate = scatter_about(key_of[5], (D, FF), D ** -0.5, 0.0625, ((1, 16),))
    w_up = scatter_about(key_of[6], (D, FF), D ** -0.5, 0.0625, ((1, 16),))
    w_down = scatter_about(key_of[7], (FF, D), FF ** -0.5, 0.0625, ((0, 16),))
    cache_keys = draw_cache_keys(jax.random.fold_in(jax.random.fold_in(key_of[11], part), 71), part)
    cache_values = scatter_about(part_keys[9], (ROWS, L, HD), 1.0, 6.0, ((0, 16),))
    lengths = draw_lengths(jax.random.fold_in(jax.random.fold_in(key_of[11], part), 71), part)
    return dict(layer_input=layer_input, norm_gain=norm_gain, w_query=w_query, w_keyval=w_keyval, w_out=w_out, w_gate=w_gate, w_up=w_up, w_down=w_down, cache_keys=cache_keys, cache_values=cache_values, lengths=lengths)


def reference(layer_input, norm_gain, w_query, w_keyval, w_out, w_gate, w_up, w_down, cache_keys, cache_values, lengths):
    widened = layer_input.astype(jnp.float32)
    row_mean = lax.optimization_barrier(jnp.mean(widened, axis=1, keepdims=True))
    centred = widened - row_mean
    row_var = lax.optimization_barrier(jnp.mean(centred * centred, axis=1, keepdims=True))
    normed = (centred * jax.lax.rsqrt(row_var + 1e-06) * norm_gain).astype(jnp.bfloat16)
    queries = jnp.dot(normed, w_query, preferred_element_type=jnp.float32).astype(jnp.bfloat16)
    keyval = jnp.dot(normed, w_keyval, preferred_element_type=jnp.float32).astype(jnp.bfloat16)
    queries = queries.reshape(ROWS, H, HD).astype(jnp.float32)
    new_key = keyval[:, :HD].astype(jnp.float32)
    new_value = keyval[:, HD:].astype(jnp.float32)
    scores = jnp.einsum('rhd,rld->rhl', queries, cache_keys.astype(jnp.float32)) / 16.0
    places = jnp.arange(L, dtype=jnp.int32)
    live_mask = places[None, :] < lengths[:, None]
    scores = jnp.where(live_mask[:, None, :], scores, -1e+30)
    own_score = jnp.einsum('rhd,rd->rh', queries, new_key) / 16.0
    highest = jnp.maximum(lax.optimization_barrier(jnp.max(scores, axis=2)), own_score)
    weights = jnp.exp(scores - highest[:, :, None])
    own_weight = jnp.exp(own_score - highest)
    denominator = lax.optimization_barrier(jnp.sum(weights, axis=2)) + own_weight
    probs = (weights / denominator[:, :, None]).astype(jnp.bfloat16).astype(jnp.float32)
    own_prob = (own_weight / denominator).astype(jnp.bfloat16).astype(jnp.float32)
    attended = jnp.einsum('rhl,rld->rhd', probs, cache_values.astype(jnp.float32))
    attended = attended + own_prob[:, :, None] * new_value[:, None, :]
    attended = attended.reshape(ROWS, H * HD).astype(jnp.bfloat16)
    gate_sum = jnp.dot(normed, w_gate, preferred_element_type=jnp.float32)
    up_sum = jnp.dot(normed, w_up, preferred_element_type=jnp.float32)
    hidden = (jax.nn.silu(gate_sum) * up_sum).astype(jnp.bfloat16)
    result = widened + jnp.dot(attended, w_out, preferred_element_type=jnp.float32)
    result = result + jnp.dot(hidden, w_down, preferred_element_type=jnp.float32)
    return result.astype(jnp.bfloat16)
```

```python
import functools

import jax
import jax.numpy as jnp
from jax import lax
from jax.experimental import pallas as pl
from jax.experimental.pallas import tpu as pltpu
from jax.sharding import PartitionSpec as P

H = 24
HD = 256
MIB = 1024 * 1024


def places(Z):
    me = lax.axis_index("gx")
    z = lax.div(me, 4)
    y = lax.rem(lax.div(me, 2), 2)
    c = lax.rem(me, 2)
    return z, y, c


def index_of(z, y, c):
    return (z * 2 + y) * 2 + c


def partners(Z, z, y, c):
    out = [index_of(lax.rem(z + d, Z), y, c) for d in range(1, Z)]
    return out + [index_of(z, 1 - y, c), index_of(z, y, 1 - c)]


def greet(Z, z, y, c):
    barrier = pltpu.get_barrier_semaphore()
    for p in partners(Z, z, y, c):
        pl.semaphore_signal(
            barrier, inc=1, device_id={"gx": p}, device_id_type=pl.DeviceIdType.MESH
        )
    return barrier


def remote(src, dst, send, recv, p):
    return pltpu.make_async_remote_copy(
        src_ref=src,
        dst_ref=dst,
        send_sem=send,
        recv_sem=recv,
        device_id={"gx": p},
        device_id_type=pl.DeviceIdType.MESH,
    )


def project_kernel(
    Z, R, C, Kc,
    x_ref, gain_ref, wq, wkv, wg, wu,
    q_out, kv_out, hid_out,
    gbuf, wqb, wkvb, wgb, wub, accq, acckv, accg, accu,
    zsend, zrecv, ysend, yrecv, csend, crecv, wsem,
):
    z, y, c = places(Z)
    barrier = greet(Z, z, y, c)
    weights = ((wq, wqb), (wkv, wkvb), (wg, wgb), (wu, wub))
    AHEAD = 4
    LY, LC = 2, 1

    def wcopy(k, i):
        src, dst = weights[i]
        return pltpu.make_async_copy(
            src.at[pl.ds(pl.multiple_of(k * Kc, Kc), Kc), :], dst.at[k], wsem.at[k, i]
        )

    def wstart(k):
        for i in range(4):
            wcopy(k, i).start()

    for k in range(min(AHEAD, C)):
        wstart(k)

    D = C * Kc
    total = jnp.zeros((R, 1), jnp.float32)
    for k in range(C):
        total += jnp.sum(x_ref[:, k * Kc : (k + 1) * Kc].astype(jnp.float32), axis=1, keepdims=True)
    mean = total / D
    square = jnp.zeros((R, 1), jnp.float32)
    for k in range(C):
        centred = x_ref[:, k * Kc : (k + 1) * Kc].astype(jnp.float32) - mean
        square += jnp.sum(centred * centred, axis=1, keepdims=True)
    scale = lax.rsqrt(square / D + 1e-06)

    line = pl.multiple_of((c * 2 + y) * Z * R, R)
    other_line = pl.multiple_of((c * 2 + 1 - y) * Z * R, R)
    half = pl.multiple_of(c * 2 * Z * R, R)
    other_half = pl.multiple_of((1 - c) * 2 * Z * R, R)
    own = pl.multiple_of(((c * 2 + y) * Z + z) * R, R)
    for k in range(C):
        cols = slice(k * Kc, (k + 1) * Kc)
        centred = x_ref[:, cols].astype(jnp.float32) - mean
        gbuf[k, pl.ds(own, R), :] = (centred * scale * gain_ref[:, cols]).astype(jnp.bfloat16)

    def zcopy(k, d):
        ref = gbuf.at[k, pl.ds(own, R), :]
        return remote(
            ref, ref, zsend.at[k, d - 1], zrecv.at[k, d - 1], index_of(lax.rem(z + d, Z), y, c)
        )

    def zarrival(k, d):
        src = pl.multiple_of(((c * 2 + y) * Z + lax.rem(z + Z - d, Z)) * R, R)
        ref = gbuf.at[k, pl.ds(src, R), :]
        return remote(
            ref, ref, zsend.at[k, d - 1], zrecv.at[k, d - 1], index_of(lax.rem(z + d, Z), y, c)
        )

    def ycopy(k, base):
        ref = gbuf.at[k, pl.ds(base, Z * R), :]
        return remote(ref, ref, ysend.at[k], yrecv.at[k], index_of(z, 1 - y, c))

    def ccopy(k, base):
        ref = gbuf.at[k, pl.ds(base, 2 * Z * R), :]
        return remote(ref, ref, csend.at[k], crecv.at[k], index_of(z, y, 1 - c))

    accq[...] = jnp.zeros_like(accq)
    acckv[...] = jnp.zeros_like(acckv)
    accg[...] = jnp.zeros_like(accg)
    accu[...] = jnp.zeros_like(accu)

    pl.semaphore_wait(barrier, Z + 1)
    for k in range(min(2, C)):
        for d in range(1, Z):
            zcopy(k, d).start()

    def step(s, carry):
        @pl.when(s + AHEAD < C)
        def _():
            wstart(s + AHEAD)

        @pl.when(s + 2 < C)
        def _():
            for d in range(1, Z):
                zcopy(s + 2, d).start()

        @pl.when(s < C)
        def _():
            for d in range(1, Z):
                zarrival(s, d).wait_recv()
            ycopy(s, line).start()

        @pl.when(jnp.logical_and(s >= LY, s < C + LY))
        def _():
            k = s - LY
            ycopy(k, other_line).wait_recv()
            ccopy(k, half).start()

        @pl.when(s >= LY + LC)
        def _():
            k = s - LY - LC
            ccopy(k, other_half).wait_recv()
            for i in range(4):
                wcopy(k, i).wait()
            rows = gbuf[k]
            for acc, w in ((accq, wqb), (acckv, wkvb), (accg, wgb), (accu, wub)):
                acc[...] += jnp.dot(rows, w[k], preferred_element_type=jnp.float32)

        return carry

    lax.fori_loop(0, C + LY + LC, step, 0)

    q_out[...] = accq[...].astype(jnp.bfloat16)
    kv_out[...] = acckv[...].astype(jnp.bfloat16)
    gate = accg[...]
    hid_out[...] = (gate * jax.nn.sigmoid(gate) * accu[...]).astype(jnp.bfloat16)

    def drain(k, carry):
        for d in range(1, Z):
            zcopy(k, d).wait_send()
        ycopy(k, line).wait_send()
        ccopy(k, half).wait_send()
        return carry

    lax.fori_loop(0, C, drain, 0)


def project(n, x, gain, wq, wkv, wg, wu):
    R, D = x.shape
    Z = n // 4
    Kc = 1024
    C = D // Kc
    N = n * R
    nq, nkv, ng = wq.shape[1], wkv.shape[1], wg.shape[1]
    vmem = pl.BlockSpec(memory_space=pltpu.VMEM)
    hbm = pl.BlockSpec(memory_space=pl.ANY)
    bf, f32 = jnp.bfloat16, jnp.float32
    return pl.pallas_call(
        functools.partial(project_kernel, Z, R, C, Kc),
        out_shape=[
            jax.ShapeDtypeStruct((N, nq), bf),
            jax.ShapeDtypeStruct((N, nkv), bf),
            jax.ShapeDtypeStruct((N, ng), bf),
        ],
        in_specs=[vmem, vmem, hbm, hbm, hbm, hbm],
        out_specs=[vmem, vmem, vmem],
        scratch_shapes=[
            pltpu.VMEM((C, N, Kc), bf),
            pltpu.VMEM((C, Kc, nq), bf),
            pltpu.VMEM((C, Kc, nkv), bf),
            pltpu.VMEM((C, Kc, ng), bf),
            pltpu.VMEM((C, Kc, ng), bf),
            pltpu.VMEM((N, nq), f32),
            pltpu.VMEM((N, nkv), f32),
            pltpu.VMEM((N, ng), f32),
            pltpu.VMEM((N, ng), f32),
            pltpu.SemaphoreType.DMA((C, Z - 1)),
            pltpu.SemaphoreType.DMA((C, Z - 1)),
            pltpu.SemaphoreType.DMA((C,)),
            pltpu.SemaphoreType.DMA((C,)),
            pltpu.SemaphoreType.DMA((C,)),
            pltpu.SemaphoreType.DMA((C,)),
            pltpu.SemaphoreType.DMA((C, 4)),
        ],
        compiler_params=pltpu.CompilerParams(
            collective_id=0, has_side_effects=True, vmem_limit_bytes=56 * MIB
        ),
        name="project",
    )(x, gain.reshape(1, D), wq, wkv, wg, wu)


def combine_kernel(
    Z, R, C, Kc,
    x_ref, lhs_ref, wo, wd,
    out_ref,
    wbuf, part, lineb, ownb, csb, crb, ysb, yrb, zsb, zrb,
    zsend, zrecv, ysend, yrecv, csend, crecv, wsem,
):
    z, y, c = places(Z)
    barrier = greet(Z, z, y, c)
    no, nd = wo.shape[0], wd.shape[0]
    AHEAD = 4
    LC, LY, LZ = 1, 2, 2

    def wcopies(k):
        cols = pl.ds(pl.multiple_of(k * Kc, Kc), Kc)
        return (
            pltpu.make_async_copy(wo.at[:, cols], wbuf.at[k, pl.ds(0, no), :], wsem.at[k, 0]),
            pltpu.make_async_copy(wd.at[:, cols], wbuf.at[k, pl.ds(no, nd), :], wsem.at[k, 1]),
        )

    def wstart(k):
        for copy in wcopies(k):
            copy.start()

    for k in range(min(AHEAD, C)):
        wstart(k)

    half = pl.multiple_of(c * 2 * Z * R, R)
    other_half = pl.multiple_of((1 - c) * 2 * Z * R, R)
    line = pl.multiple_of(y * Z * R, R)
    other_line = pl.multiple_of((1 - y) * Z * R, R)
    own = pl.multiple_of(z * R, R)

    def ccopy(k):
        return remote(csb.at[k], crb.at[k], csend.at[k], crecv.at[k], index_of(z, y, 1 - c))

    def ycopy(k):
        return remote(ysb.at[k], yrb.at[k], ysend.at[k], yrecv.at[k], index_of(z, 1 - y, c))

    def zcopy(k, d):
        to = lax.rem(z + d, Z)
        return remote(
            zsb.at[k, pl.ds(pl.multiple_of(to * R, R), R), :],
            zrb.at[k, d - 1],
            zsend.at[k, d - 1],
            zrecv.at[k, d - 1],
            index_of(to, y, c),
        )

    pl.semaphore_wait(barrier, Z + 1)

    def step(s, carry):
        @pl.when(s + AHEAD < C)
        def _():
            wstart(s + AHEAD)

        @pl.when(s < C)
        def _():
            for copy in wcopies(s):
                copy.wait()
            slot = lax.rem(s, 4)
            part[slot] = jnp.dot(lhs_ref[...], wbuf[s], preferred_element_type=jnp.float32)
            csb[s] = part[slot, pl.ds(other_half, 2 * Z * R), :].astype(jnp.bfloat16)
            ccopy(s).start()

        @pl.when(jnp.logical_and(s >= LC, s < C + LC))
        def _():
            k = s - LC
            slot = lax.rem(k, 4)
            ccopy(k).wait_recv()
            ysb[k] = (
                part[slot, pl.ds(half + other_line, Z * R), :]
                + crb[k, pl.ds(other_line, Z * R), :].astype(jnp.float32)
            ).astype(jnp.bfloat16)
            ycopy(k).start()
            lineb[slot] = part[slot, pl.ds(half + line, Z * R), :] + crb[
                k, pl.ds(line, Z * R), :
            ].astype(jnp.float32)

        @pl.when(jnp.logical_and(s >= LC + LY, s < C + LC + LY))
        def _():
            k = s - LC - LY
            slot = lax.rem(k, 4)
            ycopy(k).wait_recv()
            lineb[slot] = lineb[slot] + yrb[k].astype(jnp.float32)
            zsb[k] = lineb[slot].astype(jnp.bfloat16)
            for d in range(1, Z):
                zcopy(k, d).start()
            ownb[slot] = lineb[slot, pl.ds(own, R), :]

        @pl.when(s >= LC + LY + LZ)
        def _():
            k = s - LC - LY - LZ
            slot = lax.rem(k, 4)
            cols = pl.ds(pl.multiple_of(k * Kc, Kc), Kc)
            total = ownb[slot]
            for d in range(1, Z):
                zcopy(k, d).wait_recv()
                total = total + zrb[k, d - 1].astype(jnp.float32)
            out_ref[:, cols] = (x_ref[:, cols].astype(jnp.float32) + total).astype(jnp.bfloat16)

        return carry

    lax.fori_loop(0, C + LC + LY + LZ, step, 0)

    def drain(k, carry):
        for d in range(1, Z):
            zcopy(k, d).wait_send()
        ycopy(k).wait_send()
        ccopy(k).wait_send()
        return carry

    lax.fori_loop(0, C, drain, 0)


def combine(n, x, lhs, wo, wd):
    R, D = x.shape
    Z = n // 4
    Kc = 1024
    C = D // Kc
    N = n * R
    vmem = pl.BlockSpec(memory_space=pltpu.VMEM)
    hbm = pl.BlockSpec(memory_space=pl.ANY)
    bf, f32 = jnp.bfloat16, jnp.float32
    return pl.pallas_call(
        functools.partial(combine_kernel, Z, R, C, Kc),
        out_shape=jax.ShapeDtypeStruct((R, D), bf),
        in_specs=[vmem, vmem, hbm, hbm],
        out_specs=vmem,
        scratch_shapes=[
            pltpu.VMEM((C, lhs.shape[1], Kc), bf),
            pltpu.VMEM((4, N, Kc), f32),
            pltpu.VMEM((4, Z * R, Kc), f32),
            pltpu.VMEM((4, R, Kc), f32),
            pltpu.VMEM((C, N // 2, Kc), bf),
            pltpu.VMEM((C, N // 2, Kc), bf),
            pltpu.VMEM((C, Z * R, Kc), bf),
            pltpu.VMEM((C, Z * R, Kc), bf),
            pltpu.VMEM((C, Z * R, Kc), bf),
            pltpu.VMEM((C, Z - 1, R, Kc), bf),
            pltpu.SemaphoreType.DMA((C, Z - 1)),
            pltpu.SemaphoreType.DMA((C, Z - 1)),
            pltpu.SemaphoreType.DMA((C,)),
            pltpu.SemaphoreType.DMA((C,)),
            pltpu.SemaphoreType.DMA((C,)),
            pltpu.SemaphoreType.DMA((C,)),
            pltpu.SemaphoreType.DMA((C, 2)),
        ],
        compiler_params=pltpu.CompilerParams(
            collective_id=1, has_side_effects=True, vmem_limit_bytes=56 * MIB
        ),
        name="combine",
    )(x, lhs, wo, wd)


def block_scores(queries, key_block, lengths):
    scores = (
        jnp.einsum("rhd,rld->rhl", queries, key_block, preferred_element_type=jnp.float32) / 16.0
    )
    places = jnp.arange(key_block.shape[1], dtype=jnp.int32)
    live_mask = places[None, :] < lengths[:, None]
    return jnp.where(live_mask[:, None, :], scores, -1e30)


def attend_all(queries, new_key, new_value, cache_keys, cache_values, lengths):
    scores = block_scores(queries, cache_keys, lengths)
    own_score = (
        jnp.einsum("rhd,rd->rh", queries, new_key, preferred_element_type=jnp.float32) / 16.0
    )
    highest = jnp.maximum(jnp.max(scores, axis=2), own_score)
    weights = jnp.exp(scores - highest[:, :, None])
    own_weight = jnp.exp(own_score - highest)
    denominator = jnp.sum(weights, axis=2) + own_weight
    probs = (weights / denominator[:, :, None]).astype(jnp.bfloat16)
    own_prob = (own_weight / denominator).astype(jnp.bfloat16).astype(jnp.float32)
    attended = jnp.einsum("rhl,rld->rhd", probs, cache_values, preferred_element_type=jnp.float32)
    return attended + own_prob[:, :, None] * new_value.astype(jnp.float32)[:, None, :]


def shards(
    n,
    layer_input,
    norm_gain,
    w_query,
    w_keyval,
    w_out,
    w_gate,
    w_up,
    w_down,
    cache_keys,
    cache_values,
    lengths,
):
    R = layer_input.shape[0]
    Z = n // 4
    query_cols, keyval_cols, hidden = project(
        n, layer_input, norm_gain, w_query, w_keyval, w_gate, w_up
    )

    def to_index_order(a):
        a = a.reshape(2, 2, Z, R, a.shape[1]).transpose(2, 1, 0, 3, 4)
        return a.reshape(n, R, a.shape[4])

    query_rows, keyval_rows = (
        lax.all_to_all(to_index_order(query_cols), "gx", split_axis=0, concat_axis=0, tiled=True),
        lax.all_to_all(to_index_order(keyval_cols), "gx", split_axis=0, concat_axis=0, tiled=True),
    )
    queries = query_rows.transpose(1, 0, 2).reshape(R, H, HD)
    keyval_rows = keyval_rows.transpose(1, 0, 2).reshape(R, 2 * HD)
    new_key = keyval_rows[:, :HD]
    new_value = keyval_rows[:, HD:]
    attended = attend_all(queries, new_key, new_value, cache_keys, cache_values, lengths)
    attended = attended.reshape(R, H * HD).astype(jnp.bfloat16)
    att = lax.all_to_all(
        attended.reshape(R, n, -1).transpose(1, 0, 2), "gx", split_axis=0, concat_axis=0, tiled=True
    )
    att = att.reshape(Z, 2, 2, R, -1).transpose(2, 1, 0, 3, 4).reshape(n * R, -1)
    lhs = jnp.concatenate([att, hidden], axis=1)
    return combine(n, layer_input, lhs, w_out, w_down)


def solution(mesh):
    n = mesh.shape["gx"]
    return jax.shard_map(
        functools.partial(shards, n),
        mesh=mesh,
        in_specs=(
            P(("grp", "gx"), None),
            P(),
            P(None, "gx"),
            P(None, "gx"),
            P("gx", None),
            P(None, "gx"),
            P(None, "gx"),
            P("gx", None),
            P(("grp", "gx"), None, None),
            P(("grp", "gx"), None, None),
            P(("grp", "gx")),
        ),
        out_specs=P(("grp", "gx"), None),
        check_vma=False,
    )
```

```python
import functools

import jax
import jax.numpy as jnp
from jax import lax
from jax.experimental import pallas as pl
from jax.experimental.pallas import tpu as pltpu
from jax.sharding import PartitionSpec as P

H = 24
HD = 256
MIB = 1024 * 1024


def places(Z):
    me = lax.axis_index("gx")
    z = lax.div(me, 4)
    y = lax.rem(lax.div(me, 2), 2)
    c = lax.rem(me, 2)
    return z, y, c


def index_of(z, y, c):
    return (z * 2 + y) * 2 + c


def partners(Z, z, y, c):
    out = [index_of(lax.rem(z + d, Z), y, c) for d in range(1, Z)]
    return out + [index_of(z, 1 - y, c), index_of(z, y, 1 - c)]


def greet(Z, z, y, c, everyone=False):
    barrier = pltpu.get_barrier_semaphore()
    me = index_of(z, y, c)
    if everyone:
        all_partners = [lax.rem(me + d, 4 * Z) for d in range(1, 4 * Z)]
    else:
        all_partners = partners(Z, z, y, c)
    for p in all_partners:
        pl.semaphore_signal(
            barrier, inc=1, device_id={"gx": p}, device_id_type=pl.DeviceIdType.MESH
        )
    return barrier


def remote(src, dst, send, recv, p):
    return pltpu.make_async_remote_copy(
        src_ref=src,
        dst_ref=dst,
        send_sem=send,
        recv_sem=recv,
        device_id={"gx": p},
        device_id_type=pl.DeviceIdType.MESH,
    )


def project_kernel(
    Z, R, C, Kc,
    x_ref, gain_ref, wq, wkv, wg, wu,
    qkv_out, hid_out,
    gbuf, wqb, wkvb, wgb, wub, accq, acckv, accg, accu,
    zsend, zrecv, ysend, yrecv, csend, crecv, wsem,
):
    z, y, c = places(Z)
    barrier = greet(Z, z, y, c)
    weights = ((wq, wqb), (wkv, wkvb), (wg, wgb), (wu, wub))
    AHEAD = 4
    LY, LC = 2, 1

    def wcopy(k, i):
        src, dst = weights[i]
        part = pl.ds(pl.multiple_of(k * Kc, Kc), Kc)
        src = src.at[part, :] if i == 0 else src.at[:, part]
        return pltpu.make_async_copy(src, dst.at[k], wsem.at[k, i])

    def wstart(k):
        for i in range(4):
            wcopy(k, i).start()

    for k in range(min(AHEAD, C)):
        wstart(k)

    D = C * Kc
    total = jnp.zeros((R, 1), jnp.float32)
    for k in range(C):
        total += jnp.sum(x_ref[:, k * Kc : (k + 1) * Kc].astype(jnp.float32), axis=1, keepdims=True)
    mean = total / D
    square = jnp.zeros((R, 1), jnp.float32)
    for k in range(C):
        centred = x_ref[:, k * Kc : (k + 1) * Kc].astype(jnp.float32) - mean
        square += jnp.sum(centred * centred, axis=1, keepdims=True)
    scale = lax.rsqrt(square / D + 1e-06)

    line = pl.multiple_of((c * 2 + y) * Z * R, R)
    other_line = pl.multiple_of((c * 2 + 1 - y) * Z * R, R)
    half = pl.multiple_of(c * 2 * Z * R, R)
    other_half = pl.multiple_of((1 - c) * 2 * Z * R, R)
    own = pl.multiple_of(((c * 2 + y) * Z + z) * R, R)
    for k in range(C):
        cols = slice(k * Kc, (k + 1) * Kc)
        centred = x_ref[:, cols].astype(jnp.float32) - mean
        gbuf[k, pl.ds(own, R), :] = (centred * scale * gain_ref[:, cols]).astype(jnp.bfloat16)

    def zcopy(k, d):
        ref = gbuf.at[k, pl.ds(own, R), :]
        return remote(
            ref, ref, zsend.at[k, d - 1], zrecv.at[k, d - 1], index_of(lax.rem(z + d, Z), y, c)
        )

    def zarrival(k, d):
        src = pl.multiple_of(((c * 2 + y) * Z + lax.rem(z + Z - d, Z)) * R, R)
        ref = gbuf.at[k, pl.ds(src, R), :]
        return remote(
            ref, ref, zsend.at[k, d - 1], zrecv.at[k, d - 1], index_of(lax.rem(z + d, Z), y, c)
        )

    def ycopy(k, base):
        ref = gbuf.at[k, pl.ds(base, Z * R), :]
        return remote(ref, ref, ysend.at[k], yrecv.at[k], index_of(z, 1 - y, c))

    def ccopy(k, base):
        ref = gbuf.at[k, pl.ds(base, 2 * Z * R), :]
        return remote(ref, ref, csend.at[k], crecv.at[k], index_of(z, y, 1 - c))

    accq[...] = jnp.zeros_like(accq)
    acckv[...] = jnp.zeros_like(acckv)
    accg[...] = jnp.zeros_like(accg)
    accu[...] = jnp.zeros_like(accu)

    pl.semaphore_wait(barrier, Z + 1)
    for k in range(min(2, C)):
        for d in range(1, Z):
            zcopy(k, d).start()

    def step(s, carry):
        @pl.when(s + AHEAD < C)
        def _():
            wstart(s + AHEAD)

        @pl.when(s + 2 < C)
        def _():
            for d in range(1, Z):
                zcopy(s + 2, d).start()

        @pl.when(s < C)
        def _():
            for d in range(1, Z):
                zarrival(s, d).wait_recv()
            ycopy(s, line).start()

        @pl.when(jnp.logical_and(s >= LY, s < C + LY))
        def _():
            k = s - LY
            ycopy(k, other_line).wait_recv()
            ccopy(k, half).start()

        @pl.when(s >= LY + LC)
        def _():
            k = s - LY - LC
            ccopy(k, other_half).wait_recv()
            for i in range(4):
                wcopy(k, i).wait()
            rows = gbuf[k]
            accq[...] += jnp.dot(rows, wqb[k], preferred_element_type=jnp.float32)
            for acc, w in ((acckv, wkvb), (accg, wgb), (accu, wub)):
                acc[...] += lax.dot_general(
                    rows, w[k], (((1,), (1,)), ((), ())), preferred_element_type=jnp.float32
                )

        return carry

    lax.fori_loop(0, C + LY + LC, step, 0)

    nq, nkv, wide = accq.shape[1], acckv.shape[1], qkv_out.shape[1]
    qkv_out[...] = jnp.zeros_like(qkv_out)
    qkv_out[:, 0:nq] = accq[...].astype(jnp.bfloat16)
    qkv_out[:, wide - 128 : wide - 128 + nkv] = acckv[...].astype(jnp.bfloat16)
    gate = accg[...]
    hid_out[...] = (gate * jax.nn.sigmoid(gate) * accu[...]).astype(jnp.bfloat16)

    def drain(k, carry):
        for d in range(1, Z):
            zcopy(k, d).wait_send()
        ycopy(k, line).wait_send()
        ccopy(k, half).wait_send()
        return carry

    lax.fori_loop(0, C, drain, 0)


def project(n, x, gain, wq, wkv, wg, wu):
    R, D = x.shape
    Z = n // 4
    Kc = 1024
    C = D // Kc
    N = n * R
    nq, nkv, ng = wq.shape[1], wkv.shape[1], wg.shape[1]
    vmem = pl.BlockSpec(memory_space=pltpu.VMEM)
    hbm = pl.BlockSpec(memory_space=pl.ANY)
    bf, f32 = jnp.bfloat16, jnp.float32
    return pl.pallas_call(
        functools.partial(project_kernel, Z, R, C, Kc),
        out_shape=[
            jax.ShapeDtypeStruct((N, -(-nq // 128) * 128 + 128), bf),
            jax.ShapeDtypeStruct((N, ng), bf),
        ],
        in_specs=[vmem, vmem, hbm, hbm, hbm, hbm],
        out_specs=[vmem, vmem],
        scratch_shapes=[
            pltpu.VMEM((C, N, Kc), bf),
            pltpu.VMEM((C, Kc, nq), bf),
            pltpu.VMEM((C, nkv, Kc), bf),
            pltpu.VMEM((C, ng, Kc), bf),
            pltpu.VMEM((C, ng, Kc), bf),
            pltpu.VMEM((N, nq), f32),
            pltpu.VMEM((N, nkv), f32),
            pltpu.VMEM((N, ng), f32),
            pltpu.VMEM((N, ng), f32),
            pltpu.SemaphoreType.DMA((C, Z - 1)),
            pltpu.SemaphoreType.DMA((C, Z - 1)),
            pltpu.SemaphoreType.DMA((C,)),
            pltpu.SemaphoreType.DMA((C,)),
            pltpu.SemaphoreType.DMA((C,)),
            pltpu.SemaphoreType.DMA((C,)),
            pltpu.SemaphoreType.DMA((C, 4)),
        ],
        compiler_params=pltpu.CompilerParams(
            collective_id=0, has_side_effects=True, vmem_limit_bytes=56 * MIB
        ),
        name="project",
    )(x, gain.reshape(1, D), wq, wkv.T, wg.T, wu.T)


def attend(
    Z, R, z, y, c,
    qkv_ref, keys, values, len_ref, lhs_ref,
    qrecv, qall, score, prob, att, asend, keyb, valb,
    q_send, q_recv, a_send, a_recv, kv_sem,
    barrier,
):
    n = 4 * Z
    me = index_of(z, y, c)
    L = keyb.shape[1]
    nq = asend.shape[2]
    nkv = 2 * HD // n
    per = nq // 128
    M = H * R
    bf, f32 = jnp.bfloat16, jnp.float32
    kcopy = pltpu.make_async_copy(keys, keyb, kv_sem.at[0])
    vcopy = pltpu.make_async_copy(values, valb, kv_sem.at[1])
    kcopy.start()
    vcopy.start()

    def row_of(p):
        place = (lax.rem(p, 2) * 2 + lax.rem(lax.div(p, 2), 2)) * Z + lax.div(p, 4)
        return pl.multiple_of(place * R, R)

    def qcopy(d):
        to = lax.rem(me + d, n)
        return remote(
            qkv_ref.at[pl.ds(row_of(to), R), :], qrecv.at[me], q_send.at[d], q_recv.at[d], to
        )

    def qarrival(d):
        source = lax.rem(me + n - d, n)
        return remote(
            qkv_ref.at[pl.ds(row_of(me), R), :],
            qrecv.at[source],
            q_send.at[d],
            q_recv.at[d],
            lax.rem(me + d, n),
        )

    def acopy(d):
        to = lax.rem(me + d, n)
        return remote(
            asend.at[to],
            lhs_ref.at[pl.ds(row_of(me), R), pl.ds(0, nq)],
            a_send.at[d],
            a_recv.at[d],
            to,
        )

    def aarrival(d):
        source = lax.rem(me + n - d, n)
        return remote(
            asend.at[me],
            lhs_ref.at[pl.ds(row_of(source), R), pl.ds(0, nq)],
            a_send.at[d],
            a_recv.at[d],
            lax.rem(me + d, n),
        )

    def each(f):
        def body(d, carry):
            f(d)
            return carry

        lax.fori_loop(1, n, body, 0)

    pl.semaphore_wait(barrier, n - 1)
    each(lambda d: qcopy(d).start())
    qrecv[me] = qkv_ref[pl.ds(row_of(me), R), :]
    each(lambda d: qarrival(d).wait_recv())

    for b in range(2 * H):
        qall[(b // 2) * R : (b // 2 + 1) * R, (b % 2) * 128 : (b % 2 + 1) * 128] = qrecv[
            b // per, :, (b % per) * 128 : (b % per + 1) * 128
        ]
    wide = qrecv.shape[2]
    pieces = [qrecv[p, :, wide - 128 :].astype(f32)[:, :nkv] for p in range(n)]
    new_key = jnp.concatenate(pieces[: n // 2], axis=1)
    new_value = jnp.concatenate(pieces[n // 2 :], axis=1)

    row_in_head = lax.rem(lax.broadcasted_iota(jnp.int32, (M, L), 0), R)
    kcopy.wait()

    def score_row(r, carry):
        s = lax.dot_general(
            qall[...], keyb[r], (((1,), (1,)), ((), ())), preferred_element_type=f32
        )
        score[...] = jnp.where(row_in_head == r, s, score[...])
        return carry

    score[...] = jnp.zeros_like(score)
    lax.fori_loop(0, R, score_row, 0)

    live = lax.broadcasted_iota(jnp.int32, (R, L), 1) < len_ref[...]
    for h in range(H):
        rows = slice(h * R, (h + 1) * R)
        s = jnp.where(live, score[rows, :] / 16.0, -1e30)
        own = jnp.sum(qall[rows, :].astype(f32) * new_key, axis=1, keepdims=True) / 16.0
        highest = jnp.maximum(jnp.max(s, axis=1, keepdims=True), own)
        weights = jnp.exp(s - highest)
        own_weight = jnp.exp(own - highest)
        denominator = jnp.sum(weights, axis=1, keepdims=True) + own_weight
        prob[rows, :] = (weights / denominator).astype(bf).astype(f32)
        own_prob = (own_weight / denominator).astype(bf).astype(f32)
        att[rows, :] = own_prob * new_value

    vcopy.wait()

    def value_row(r, carry):
        p = jnp.where(row_in_head == r, prob[...], 0.0).astype(bf)
        att[...] += jnp.dot(p, valb[r], preferred_element_type=f32)
        return carry

    lax.fori_loop(0, R, value_row, 0)

    for b in range(2 * H):
        asend[b // per, :, (b % per) * 128 : (b % per + 1) * 128] = att[
            (b // 2) * R : (b // 2 + 1) * R, (b % 2) * 128 : (b % 2 + 1) * 128
        ].astype(bf)
    each(lambda d: acopy(d).start())
    lhs_ref[pl.ds(row_of(me), R), pl.ds(0, nq)] = asend[me]
    each(lambda d: aarrival(d).wait_recv())

    def drain():
        each(lambda d: qcopy(d).wait_send())
        each(lambda d: acopy(d).wait_send())

    return drain


def combine_kernel(
    Z, R, C, Kc, fused,
    x_ref, *refs,
):
    if fused:
        qkv_ref, hid_ref, keys, values, len_ref, wo, wd, out_ref, lhs_ref = refs[:9]
        attend_scratch = refs[9:22]
        refs = refs[22:]
    else:
        lhs_ref, wo, wd, out_ref = refs[:4]
        refs = refs[4:]
    (
        wbuf, part, lineb, ownb, csb, crb, ysb, yrb, zsb, zrb,
        zsend, zrecv, ysend, yrecv, csend, crecv, wsem,
    ) = refs
    z, y, c = places(Z)
    barrier = greet(Z, z, y, c, fused)
    no, nd = wo.shape[0], wd.shape[0]
    AHEAD = 4
    LC, LY, LZ = 1, 2, 2

    def wcopies(k):
        cols = pl.ds(pl.multiple_of(k * Kc, Kc), Kc)
        return (
            pltpu.make_async_copy(wo.at[:, cols], wbuf.at[k, pl.ds(0, no), :], wsem.at[k, 0]),
            pltpu.make_async_copy(wd.at[:, cols], wbuf.at[k, pl.ds(no, nd), :], wsem.at[k, 1]),
        )

    def wstart(k):
        for copy in wcopies(k):
            copy.start()

    for k in range(min(AHEAD, C)):
        wstart(k)

    half = pl.multiple_of(c * 2 * Z * R, R)
    other_half = pl.multiple_of((1 - c) * 2 * Z * R, R)
    line = pl.multiple_of(y * Z * R, R)
    other_line = pl.multiple_of((1 - y) * Z * R, R)
    own = pl.multiple_of(z * R, R)

    def ccopy(k):
        return remote(csb.at[k], crb.at[k], csend.at[k], crecv.at[k], index_of(z, y, 1 - c))

    def ycopy(k):
        return remote(ysb.at[k], yrb.at[k], ysend.at[k], yrecv.at[k], index_of(z, 1 - y, c))

    def zcopy(k, d):
        to = lax.rem(z + d, Z)
        return remote(
            zsb.at[k, pl.ds(pl.multiple_of(to * R, R), R), :],
            zrb.at[k, d - 1],
            zsend.at[k, d - 1],
            zrecv.at[k, d - 1],
            index_of(to, y, c),
        )

    if fused:
        lhs_ref[:, no:] = hid_ref[...]
        finish = attend(
            Z, R, z, y, c, qkv_ref, keys, values, len_ref, lhs_ref, *attend_scratch, barrier
        )
    else:
        pl.semaphore_wait(barrier, Z + 1)

    def step(s, carry):
        @pl.when(s + AHEAD < C)
        def _():
            wstart(s + AHEAD)

        @pl.when(s < C)
        def _():
            for copy in wcopies(s):
                copy.wait()
            slot = lax.rem(s, 4)
            part[slot] = jnp.dot(lhs_ref[...], wbuf[s], preferred_element_type=jnp.float32)
            csb[s] = part[slot, pl.ds(other_half, 2 * Z * R), :].astype(jnp.bfloat16)
            ccopy(s).start()

        @pl.when(jnp.logical_and(s >= LC, s < C + LC))
        def _():
            k = s - LC
            slot = lax.rem(k, 4)
            ccopy(k).wait_recv()
            ysb[k] = (
                part[slot, pl.ds(half + other_line, Z * R), :]
                + crb[k, pl.ds(other_line, Z * R), :].astype(jnp.float32)
            ).astype(jnp.bfloat16)
            ycopy(k).start()
            lineb[slot] = part[slot, pl.ds(half + line, Z * R), :] + crb[
                k, pl.ds(line, Z * R), :
            ].astype(jnp.float32)

        @pl.when(jnp.logical_and(s >= LC + LY, s < C + LC + LY))
        def _():
            k = s - LC - LY
            slot = lax.rem(k, 4)
            ycopy(k).wait_recv()
            lineb[slot] = lineb[slot] + yrb[k].astype(jnp.float32)
            zsb[k] = lineb[slot].astype(jnp.bfloat16)
            for d in range(1, Z):
                zcopy(k, d).start()
            ownb[slot] = lineb[slot, pl.ds(own, R), :]

        @pl.when(s >= LC + LY + LZ)
        def _():
            k = s - LC - LY - LZ
            slot = lax.rem(k, 4)
            cols = pl.ds(pl.multiple_of(k * Kc, Kc), Kc)
            total = ownb[slot]
            for d in range(1, Z):
                zcopy(k, d).wait_recv()
                total = total + zrb[k, d - 1].astype(jnp.float32)
            out_ref[:, cols] = (x_ref[:, cols].astype(jnp.float32) + total).astype(jnp.bfloat16)

        return carry

    lax.fori_loop(0, C + LC + LY + LZ, step, 0)

    def drain(k, carry):
        for d in range(1, Z):
            zcopy(k, d).wait_send()
        ycopy(k).wait_send()
        ccopy(k).wait_send()
        return carry

    lax.fori_loop(0, C, drain, 0)
    if fused:
        finish()


def combine(n, x, operands, wo, wd):
    fused = len(operands) > 1
    R, D = x.shape
    Z = n // 4
    Kc = 1024
    C = D // Kc
    N = n * R
    vmem = pl.BlockSpec(memory_space=pltpu.VMEM)
    hbm = pl.BlockSpec(memory_space=pl.ANY)
    bf, f32 = jnp.bfloat16, jnp.float32
    nq, nin = wo.shape[0], wo.shape[0] + wd.shape[0]
    extra = []
    if fused:
        qkv, _, keys, _, _ = operands
        L = keys.shape[1]
        extra = [
            pltpu.VMEM((N, nin), bf),
            pltpu.VMEM((n, R, qkv.shape[1]), bf),
            pltpu.VMEM((H * R, HD), bf),
            pltpu.VMEM((H * R, L), f32),
            pltpu.VMEM((H * R, L), f32),
            pltpu.VMEM((H * R, HD), f32),
            pltpu.VMEM((n, R, nq), bf),
            pltpu.VMEM((R, L, HD), bf),
            pltpu.VMEM((R, L, HD), bf),
            pltpu.SemaphoreType.DMA((n,)),
            pltpu.SemaphoreType.DMA((n,)),
            pltpu.SemaphoreType.DMA((n,)),
            pltpu.SemaphoreType.DMA((n,)),
            pltpu.SemaphoreType.DMA((2,)),
        ]
    return pl.pallas_call(
        functools.partial(combine_kernel, Z, R, C, Kc, fused),
        out_shape=jax.ShapeDtypeStruct((R, D), bf),
        in_specs=[vmem] + ([vmem, vmem, hbm, hbm, vmem] if fused else [vmem]) + [hbm, hbm],
        out_specs=vmem,
        scratch_shapes=extra
        + [
            pltpu.VMEM((C, nin, Kc), bf),
            pltpu.VMEM((4, N, Kc), f32),
            pltpu.VMEM((4, Z * R, Kc), f32),
            pltpu.VMEM((4, R, Kc), f32),
            pltpu.VMEM((C, N // 2, Kc), bf),
            pltpu.VMEM((C, N // 2, Kc), bf),
            pltpu.VMEM((C, Z * R, Kc), bf),
            pltpu.VMEM((C, Z * R, Kc), bf),
            pltpu.VMEM((C, Z * R, Kc), bf),
            pltpu.VMEM((C, Z - 1, R, Kc), bf),
            pltpu.SemaphoreType.DMA((C, Z - 1)),
            pltpu.SemaphoreType.DMA((C, Z - 1)),
            pltpu.SemaphoreType.DMA((C,)),
            pltpu.SemaphoreType.DMA((C,)),
            pltpu.SemaphoreType.DMA((C,)),
            pltpu.SemaphoreType.DMA((C,)),
            pltpu.SemaphoreType.DMA((C, 2)),
        ],
        compiler_params=pltpu.CompilerParams(
            collective_id=1, has_side_effects=True, vmem_limit_bytes=56 * MIB
        ),
        name="combine",
    )(x, *operands, wo, wd)


def block_scores(queries, key_block, lengths):
    scores = (
        jnp.einsum("rhd,rld->rhl", queries, key_block, preferred_element_type=jnp.float32) / 16.0
    )
    places = jnp.arange(key_block.shape[1], dtype=jnp.int32)
    live_mask = places[None, :] < lengths[:, None]
    return jnp.where(live_mask[:, None, :], scores, -1e30)


def attend_all(queries, new_key, new_value, cache_keys, cache_values, lengths):
    scores = block_scores(queries, cache_keys, lengths)
    own_score = (
        jnp.einsum("rhd,rd->rh", queries, new_key, preferred_element_type=jnp.float32) / 16.0
    )
    highest = jnp.maximum(jnp.max(scores, axis=2), own_score)
    weights = jnp.exp(scores - highest[:, :, None])
    own_weight = jnp.exp(own_score - highest)
    denominator = jnp.sum(weights, axis=2) + own_weight
    probs = (weights / denominator[:, :, None]).astype(jnp.bfloat16)
    own_prob = (own_weight / denominator).astype(jnp.bfloat16).astype(jnp.float32)
    attended = jnp.einsum("rhl,rld->rhd", probs, cache_values, preferred_element_type=jnp.float32)
    return attended + own_prob[:, :, None] * new_value.astype(jnp.float32)[:, None, :]


def shards(
    n,
    layer_input,
    norm_gain,
    w_query,
    w_keyval,
    w_out,
    w_gate,
    w_up,
    w_down,
    cache_keys,
    cache_values,
    lengths,
):
    R = layer_input.shape[0]
    Z = n // 4
    qkv, hidden = project(n, layer_input, norm_gain, w_query, w_keyval, w_gate, w_up)
    nq, nkv = w_query.shape[1], w_keyval.shape[1]
    if nq % 128 == 0 and w_out.shape[0] == nq:
        operands = (qkv, hidden, cache_keys, cache_values, lengths.reshape(R, 1))
        return combine(n, layer_input, operands, w_out, w_down)
    query_cols = qkv[:, :nq]
    keyval_cols = qkv[:, qkv.shape[1] - 128 :][:, :nkv]

    def to_index_order(a):
        a = a.reshape(2, 2, Z, R, a.shape[1]).transpose(2, 1, 0, 3, 4)
        return a.reshape(n, R, a.shape[4])

    query_rows, keyval_rows = (
        lax.all_to_all(to_index_order(query_cols), "gx", split_axis=0, concat_axis=0, tiled=True),
        lax.all_to_all(to_index_order(keyval_cols), "gx", split_axis=0, concat_axis=0, tiled=True),
    )
    queries = query_rows.transpose(1, 0, 2).reshape(R, H, HD)
    keyval_rows = keyval_rows.transpose(1, 0, 2).reshape(R, 2 * HD)
    new_key = keyval_rows[:, :HD]
    new_value = keyval_rows[:, HD:]
    attended = attend_all(queries, new_key, new_value, cache_keys, cache_values, lengths)
    attended = attended.reshape(R, H * HD).astype(jnp.bfloat16)
    att = lax.all_to_all(
        attended.reshape(R, n, -1).transpose(1, 0, 2), "gx", split_axis=0, concat_axis=0, tiled=True
    )
    att = att.reshape(Z, 2, 2, R, -1).transpose(2, 1, 0, 3, 4).reshape(n * R, -1)
    lhs = jnp.concatenate([att, hidden], axis=1)
    return combine(n, layer_input, (lhs,), w_out, w_down)


def solution(mesh):
    n = mesh.shape["gx"]
    return jax.shard_map(
        functools.partial(shards, n),
        mesh=mesh,
        in_specs=(
            P(("grp", "gx"), None),
            P(),
            P(None, "gx"),
            P(None, "gx"),
            P("gx", None),
            P(None, "gx"),
            P(None, "gx"),
            P("gx", None),
            P(("grp", "gx"), None, None),
            P(("grp", "gx"), None, None),
            P(("grp", "gx")),
        ),
        out_specs=P(("grp", "gx"), None),
        check_vma=False,
    )
```

```python
import functools

import jax
import jax.numpy as jnp
from jax import lax
from jax.experimental import pallas as pl
from jax.experimental.pallas import tpu as pltpu
from jax.sharding import PartitionSpec as P

H = 24
HD = 256
MIB = 1024 * 1024


def places(Z):
    me = lax.axis_index("gx")
    z = lax.div(me, 4)
    y = lax.rem(lax.div(me, 2), 2)
    c = lax.rem(me, 2)
    return z, y, c


def index_of(z, y, c):
    return (z * 2 + y) * 2 + c


def partners(Z, z, y, c):
    out = [index_of(lax.rem(z + d, Z), y, c) for d in range(1, Z)]
    return out + [index_of(z, 1 - y, c), index_of(z, y, 1 - c)]


def greet(Z, z, y, c, everyone=False):
    barrier = pltpu.get_barrier_semaphore()
    me = index_of(z, y, c)
    if everyone:
        all_partners = [lax.rem(me + d, 4 * Z) for d in range(1, 4 * Z)]
    else:
        all_partners = partners(Z, z, y, c)
    for p in all_partners:
        pl.semaphore_signal(
            barrier, inc=1, device_id={"gx": p}, device_id_type=pl.DeviceIdType.MESH
        )
    return barrier


def remote(src, dst, send, recv, p):
    return pltpu.make_async_remote_copy(
        src_ref=src,
        dst_ref=dst,
        send_sem=send,
        recv_sem=recv,
        device_id={"gx": p},
        device_id_type=pl.DeviceIdType.MESH,
    )


def project_kernel(
    Z, R, C, Kc,
    x_ref, gain_ref, wq, wkv, wg, wu,
    qkv_out, hid_out,
    gbuf, wqb, wkvb, wgb, wub, accq, acckv, accg, accu,
    zsend, zrecv, ysend, yrecv, csend, crecv, wsem,
):
    z, y, c = places(Z)
    barrier = greet(Z, z, y, c)
    weights = ((wq, wqb), (wkv, wkvb), (wg, wgb), (wu, wub))
    AHEAD = 4
    LY, LC = 2, 1

    def wcopy(k, i):
        src, dst = weights[i]
        part = pl.ds(pl.multiple_of(k * Kc, Kc), Kc)
        src = src.at[part, :] if i == 0 else src.at[:, part]
        return pltpu.make_async_copy(src, dst.at[k], wsem.at[k, i])

    def wstart(k):
        for i in range(4):
            wcopy(k, i).start()

    for k in range(min(AHEAD, C)):
        wstart(k)

    D = C * Kc
    total = jnp.zeros((R, 1), jnp.float32)
    for k in range(C):
        total += jnp.sum(x_ref[:, k * Kc : (k + 1) * Kc].astype(jnp.float32), axis=1, keepdims=True)
    mean = total / D
    square = jnp.zeros((R, 1), jnp.float32)
    for k in range(C):
        centred = x_ref[:, k * Kc : (k + 1) * Kc].astype(jnp.float32) - mean
        square += jnp.sum(centred * centred, axis=1, keepdims=True)
    scale = lax.rsqrt(square / D + 1e-06)

    line = pl.multiple_of((c * 2 + y) * Z * R, R)
    other_line = pl.multiple_of((c * 2 + 1 - y) * Z * R, R)
    half = pl.multiple_of(c * 2 * Z * R, R)
    other_half = pl.multiple_of((1 - c) * 2 * Z * R, R)
    own = pl.multiple_of(((c * 2 + y) * Z + z) * R, R)
    for k in range(C):
        cols = slice(k * Kc, (k + 1) * Kc)
        centred = x_ref[:, cols].astype(jnp.float32) - mean
        gbuf[k, pl.ds(own, R), :] = (centred * scale * gain_ref[:, cols]).astype(jnp.bfloat16)

    def zcopy(k, d):
        ref = gbuf.at[k, pl.ds(own, R), :]
        return remote(
            ref, ref, zsend.at[k, d - 1], zrecv.at[k, d - 1], index_of(lax.rem(z + d, Z), y, c)
        )

    def zarrival(k, d):
        src = pl.multiple_of(((c * 2 + y) * Z + lax.rem(z + Z - d, Z)) * R, R)
        ref = gbuf.at[k, pl.ds(src, R), :]
        return remote(
            ref, ref, zsend.at[k, d - 1], zrecv.at[k, d - 1], index_of(lax.rem(z + d, Z), y, c)
        )

    def ycopy(k, base):
        ref = gbuf.at[k, pl.ds(base, Z * R), :]
        return remote(ref, ref, ysend.at[k], yrecv.at[k], index_of(z, 1 - y, c))

    def ccopy(k, base):
        ref = gbuf.at[k, pl.ds(base, 2 * Z * R), :]
        return remote(ref, ref, csend.at[k], crecv.at[k], index_of(z, y, 1 - c))

    accq[...] = jnp.zeros_like(accq)
    acckv[...] = jnp.zeros_like(acckv)
    accg[...] = jnp.zeros_like(accg)
    accu[...] = jnp.zeros_like(accu)

    pl.semaphore_wait(barrier, Z + 1)
    for k in range(min(2, C)):
        for d in range(1, Z):
            zcopy(k, d).start()

    def step(s, carry):
        @pl.when(s + AHEAD < C)
        def _():
            wstart(s + AHEAD)

        @pl.when(s + 2 < C)
        def _():
            for d in range(1, Z):
                zcopy(s + 2, d).start()

        @pl.when(s < C)
        def _():
            for d in range(1, Z):
                zarrival(s, d).wait_recv()
            ycopy(s, line).start()

        @pl.when(jnp.logical_and(s >= LY, s < C + LY))
        def _():
            k = s - LY
            ycopy(k, other_line).wait_recv()
            ccopy(k, half).start()

        @pl.when(s >= LY + LC)
        def _():
            k = s - LY - LC
            ccopy(k, other_half).wait_recv()
            for i in range(4):
                wcopy(k, i).wait()
            rows = gbuf[k]
            accq[...] += jnp.dot(rows, wqb[k], preferred_element_type=jnp.float32)
            for acc, w in ((acckv, wkvb), (accg, wgb), (accu, wub)):
                acc[...] += lax.dot_general(
                    rows, w[k], (((1,), (1,)), ((), ())), preferred_element_type=jnp.float32
                )

        return carry

    lax.fori_loop(0, C + LY + LC, step, 0)

    nq, nkv, wide = accq.shape[1], acckv.shape[1], qkv_out.shape[1]
    qkv_out[...] = jnp.zeros_like(qkv_out)
    qkv_out[:, 0:nq] = accq[...].astype(jnp.bfloat16)
    qkv_out[:, wide - 128 : wide - 128 + nkv] = acckv[...].astype(jnp.bfloat16)
    gate = accg[...]
    hid_out[...] = (gate * jax.nn.sigmoid(gate) * accu[...]).astype(jnp.bfloat16)

    def drain(k, carry):
        for d in range(1, Z):
            zcopy(k, d).wait_send()
        ycopy(k, line).wait_send()
        ccopy(k, half).wait_send()
        return carry

    lax.fori_loop(0, C, drain, 0)


def project(n, x, gain, wq, wkv, wg, wu):
    R, D = x.shape
    Z = n // 4
    Kc = 1024
    C = D // Kc
    N = n * R
    nq, nkv, ng = wq.shape[1], wkv.shape[1], wg.shape[1]
    vmem = pl.BlockSpec(memory_space=pltpu.VMEM)
    hbm = pl.BlockSpec(memory_space=pl.ANY)
    bf, f32 = jnp.bfloat16, jnp.float32
    return pl.pallas_call(
        functools.partial(project_kernel, Z, R, C, Kc),
        out_shape=[
            jax.ShapeDtypeStruct((N, -(-nq // 128) * 128 + 128), bf),
            jax.ShapeDtypeStruct((N, ng), bf),
        ],
        in_specs=[vmem, vmem, hbm, hbm, hbm, hbm],
        out_specs=[vmem, vmem],
        scratch_shapes=[
            pltpu.VMEM((C, N, Kc), bf),
            pltpu.VMEM((C, Kc, nq), bf),
            pltpu.VMEM((C, nkv, Kc), bf),
            pltpu.VMEM((C, ng, Kc), bf),
            pltpu.VMEM((C, ng, Kc), bf),
            pltpu.VMEM((N, nq), f32),
            pltpu.VMEM((N, nkv), f32),
            pltpu.VMEM((N, ng), f32),
            pltpu.VMEM((N, ng), f32),
            pltpu.SemaphoreType.DMA((C, Z - 1)),
            pltpu.SemaphoreType.DMA((C, Z - 1)),
            pltpu.SemaphoreType.DMA((C,)),
            pltpu.SemaphoreType.DMA((C,)),
            pltpu.SemaphoreType.DMA((C,)),
            pltpu.SemaphoreType.DMA((C,)),
            pltpu.SemaphoreType.DMA((C, 4)),
        ],
        compiler_params=pltpu.CompilerParams(
            collective_id=0, has_side_effects=True, vmem_limit_bytes=56 * MIB
        ),
        name="project",
    )(x, gain.reshape(1, D), wq, wkv.T, wg.T, wu.T)


def attend(
    Z, R, z, y, c,
    qkv_ref, keys, values, len_ref, lhs_ref,
    qrecv, qall, score, prob, att, asend, keyb, valb,
    q_send, q_recv, a_send, a_recv, kv_sem,
    barrier,
):
    n = 4 * Z
    me = index_of(z, y, c)
    L = keyb.shape[1]
    nq = asend.shape[2]
    nkv = 2 * HD // n
    per = nq // 128
    M = H * R
    bf, f32 = jnp.bfloat16, jnp.float32
    kcopy = pltpu.make_async_copy(keys, keyb, kv_sem.at[0])
    vcopy = pltpu.make_async_copy(values, valb, kv_sem.at[1])
    kcopy.start()
    vcopy.start()

    def row_of(p):
        place = (lax.rem(p, 2) * 2 + lax.rem(lax.div(p, 2), 2)) * Z + lax.div(p, 4)
        return pl.multiple_of(place * R, R)

    def qcopy(d):
        to = lax.rem(me + d, n)
        return remote(
            qkv_ref.at[pl.ds(row_of(to), R), :], qrecv.at[me], q_send.at[d], q_recv.at[d], to
        )

    def qarrival(d):
        source = lax.rem(me + n - d, n)
        return remote(
            qkv_ref.at[pl.ds(row_of(me), R), :],
            qrecv.at[source],
            q_send.at[d],
            q_recv.at[d],
            lax.rem(me + d, n),
        )

    def acopy(d):
        to = lax.rem(me + d, n)
        return remote(
            asend.at[to],
            lhs_ref.at[pl.ds(row_of(me), R), pl.ds(0, nq)],
            a_send.at[d],
            a_recv.at[d],
            to,
        )

    def aarrival(d):
        source = lax.rem(me + n - d, n)
        return remote(
            asend.at[me],
            lhs_ref.at[pl.ds(row_of(source), R), pl.ds(0, nq)],
            a_send.at[d],
            a_recv.at[d],
            lax.rem(me + d, n),
        )

    def each(f):
        for d in sorted(range(1, n), key=lambda d: abs(n - 2 * d)):
            f(d)

    pl.semaphore_wait(barrier, n - 1)
    each(lambda d: qcopy(d).start())
    qrecv[me] = qkv_ref[pl.ds(row_of(me), R), :]
    each(lambda d: qarrival(d).wait_recv())

    for b in range(2 * H):
        qall[(b // 2) * R : (b // 2 + 1) * R, (b % 2) * 128 : (b % 2 + 1) * 128] = qrecv[
            b // per, :, (b % per) * 128 : (b % per + 1) * 128
        ]
    wide = qrecv.shape[2]
    pieces = [qrecv[p, :, wide - 128 :].astype(f32)[:, :nkv] for p in range(n)]
    new_key = jnp.concatenate(pieces[: n // 2], axis=1)
    new_value = jnp.concatenate(pieces[n // 2 :], axis=1)

    row_in_head = lax.rem(lax.broadcasted_iota(jnp.int32, (M, L), 0), R)
    kcopy.wait()

    def score_rows(i, carry):
        picked = score[...]
        for j in range(4):
            r = i * 4 + j
            s = lax.dot_general(
                qall[...], keyb[r], (((1,), (1,)), ((), ())), preferred_element_type=f32
            )
            picked = jnp.where(row_in_head == r, s, picked)
        score[...] = picked
        return carry

    score[...] = jnp.zeros_like(score)
    lax.fori_loop(0, R // 4, score_rows, 0)

    row = lax.broadcasted_iota(jnp.int32, (R, L), 0)
    length = jnp.zeros((R, L), jnp.int32)
    for r in range(R):
        length = jnp.where(row == r, len_ref[r], length)
    live = lax.broadcasted_iota(jnp.int32, (R, L), 1) < length
    for h in range(H):
        rows = slice(h * R, (h + 1) * R)
        s = jnp.where(live, score[rows, :] / 16.0, -1e30)
        own = jnp.sum(qall[rows, :].astype(f32) * new_key, axis=1, keepdims=True) / 16.0
        highest = jnp.maximum(jnp.max(s, axis=1, keepdims=True), own)
        weights = jnp.exp(s - highest)
        own_weight = jnp.exp(own - highest)
        denominator = jnp.sum(weights, axis=1, keepdims=True) + own_weight
        prob[rows, :] = (weights / denominator).astype(bf).astype(f32)
        own_prob = (own_weight / denominator).astype(bf).astype(f32)
        att[rows, :] = own_prob * new_value

    vcopy.wait()

    def value_rows(i, carry):
        total = att[...]
        for j in range(4):
            r = i * 4 + j
            p = jnp.where(row_in_head == r, prob[...], 0.0).astype(bf)
            total = total + jnp.dot(p, valb[r], preferred_element_type=f32)
        att[...] = total
        return carry

    lax.fori_loop(0, R // 4, value_rows, 0)

    for b in range(2 * H):
        asend[b // per, :, (b % per) * 128 : (b % per + 1) * 128] = att[
            (b // 2) * R : (b // 2 + 1) * R, (b % 2) * 128 : (b % 2 + 1) * 128
        ].astype(bf)
    each(lambda d: acopy(d).start())
    lhs_ref[pl.ds(row_of(me), R), pl.ds(0, nq)] = asend[me]
    each(lambda d: aarrival(d).wait_recv())

    def drain():
        each(lambda d: qcopy(d).wait_send())
        each(lambda d: acopy(d).wait_send())

    return drain


def combine_kernel(
    Z, R, C, Kc, fused,
    x_ref, *refs,
):
    if fused:
        qkv_ref, hid_ref, keys, values, len_ref, wo, wd, out_ref, lhs_ref = refs[:9]
        attend_scratch = refs[9:22]
        refs = refs[22:]
    else:
        lhs_ref, wo, wd, out_ref = refs[:4]
        refs = refs[4:]
    (
        wbuf, part, lineb, ownb, csb, crb, ysb, yrb, zsb, zrb,
        zsend, zrecv, ysend, yrecv, csend, crecv, wsem,
    ) = refs
    z, y, c = places(Z)
    barrier = greet(Z, z, y, c, fused)
    no, nd = wo.shape[0], wd.shape[0]
    AHEAD = 4
    LC, LY, LZ = 1, 2, 2

    def wcopies(k):
        cols = pl.ds(pl.multiple_of(k * Kc, Kc), Kc)
        return (
            pltpu.make_async_copy(wo.at[:, cols], wbuf.at[k, pl.ds(0, no), :], wsem.at[k, 0]),
            pltpu.make_async_copy(wd.at[:, cols], wbuf.at[k, pl.ds(no, nd), :], wsem.at[k, 1]),
        )

    def wstart(k):
        for copy in wcopies(k):
            copy.start()

    for k in range(min(AHEAD, C)):
        wstart(k)

    half = pl.multiple_of(c * 2 * Z * R, R)
    other_half = pl.multiple_of((1 - c) * 2 * Z * R, R)
    line = pl.multiple_of(y * Z * R, R)
    other_line = pl.multiple_of((1 - y) * Z * R, R)
    own = pl.multiple_of(z * R, R)

    def ccopy(k):
        return remote(csb.at[k], crb.at[k], csend.at[k], crecv.at[k], index_of(z, y, 1 - c))

    def ycopy(k):
        return remote(ysb.at[k], yrb.at[k], ysend.at[k], yrecv.at[k], index_of(z, 1 - y, c))

    def zcopy(k, d):
        to = lax.rem(z + d, Z)
        return remote(
            zsb.at[k, pl.ds(pl.multiple_of(to * R, R), R), :],
            zrb.at[k, d - 1],
            zsend.at[k, d - 1],
            zrecv.at[k, d - 1],
            index_of(to, y, c),
        )

    if fused:
        lhs_ref[:, no:] = hid_ref[...]
        finish = attend(
            Z, R, z, y, c, qkv_ref, keys, values, len_ref, lhs_ref, *attend_scratch, barrier
        )
    else:
        pl.semaphore_wait(barrier, Z + 1)

    def step(s, carry):
        @pl.when(s + AHEAD < C)
        def _():
            wstart(s + AHEAD)

        @pl.when(s < C)
        def _():
            for copy in wcopies(s):
                copy.wait()
            slot = lax.rem(s, 4)
            part[slot] = jnp.dot(lhs_ref[...], wbuf[s], preferred_element_type=jnp.float32)
            csb[s] = part[slot, pl.ds(other_half, 2 * Z * R), :].astype(jnp.bfloat16)
            ccopy(s).start()

        @pl.when(jnp.logical_and(s >= LC, s < C + LC))
        def _():
            k = s - LC
            slot = lax.rem(k, 4)
            ccopy(k).wait_recv()
            ysb[k] = (
                part[slot, pl.ds(half + other_line, Z * R), :]
                + crb[k, pl.ds(other_line, Z * R), :].astype(jnp.float32)
            ).astype(jnp.bfloat16)
            ycopy(k).start()
            lineb[slot] = part[slot, pl.ds(half + line, Z * R), :] + crb[
                k, pl.ds(line, Z * R), :
            ].astype(jnp.float32)

        @pl.when(jnp.logical_and(s >= LC + LY, s < C + LC + LY))
        def _():
            k = s - LC - LY
            slot = lax.rem(k, 4)
            ycopy(k).wait_recv()
            lineb[slot] = lineb[slot] + yrb[k].astype(jnp.float32)
            zsb[k] = lineb[slot].astype(jnp.bfloat16)
            for d in range(1, Z):
                zcopy(k, d).start()
            ownb[slot] = lineb[slot, pl.ds(own, R), :]

        @pl.when(s >= LC + LY + LZ)
        def _():
            k = s - LC - LY - LZ
            slot = lax.rem(k, 4)
            cols = pl.ds(pl.multiple_of(k * Kc, Kc), Kc)
            total = ownb[slot]
            for d in range(1, Z):
                zcopy(k, d).wait_recv()
                total = total + zrb[k, d - 1].astype(jnp.float32)
            out_ref[:, cols] = (x_ref[:, cols].astype(jnp.float32) + total).astype(jnp.bfloat16)

        return carry

    lax.fori_loop(0, C + LC + LY + LZ, step, 0)

    def drain(k, carry):
        for d in range(1, Z):
            zcopy(k, d).wait_send()
        ycopy(k).wait_send()
        ccopy(k).wait_send()
        return carry

    lax.fori_loop(0, C, drain, 0)
    if fused:
        finish()


def combine(n, x, operands, wo, wd):
    fused = len(operands) > 1
    R, D = x.shape
    Z = n // 4
    Kc = 1024
    C = D // Kc
    N = n * R
    vmem = pl.BlockSpec(memory_space=pltpu.VMEM)
    hbm = pl.BlockSpec(memory_space=pl.ANY)
    smem = pl.BlockSpec(memory_space=pltpu.SMEM)
    bf, f32 = jnp.bfloat16, jnp.float32
    nq, nin = wo.shape[0], wo.shape[0] + wd.shape[0]
    extra = []
    if fused:
        qkv, _, keys, _, _ = operands
        L = keys.shape[1]
        extra = [
            pltpu.VMEM((N, nin), bf),
            pltpu.VMEM((n, R, qkv.shape[1]), bf),
            pltpu.VMEM((H * R, HD), bf),
            pltpu.VMEM((H * R, L), f32),
            pltpu.VMEM((H * R, L), f32),
            pltpu.VMEM((H * R, HD), f32),
            pltpu.VMEM((n, R, nq), bf),
            pltpu.VMEM((R, L, HD), bf),
            pltpu.VMEM((R, L, HD), bf),
            pltpu.SemaphoreType.DMA((n,)),
            pltpu.SemaphoreType.DMA((n,)),
            pltpu.SemaphoreType.DMA((n,)),
            pltpu.SemaphoreType.DMA((n,)),
            pltpu.SemaphoreType.DMA((2,)),
        ]
    return pl.pallas_call(
        functools.partial(combine_kernel, Z, R, C, Kc, fused),
        out_shape=jax.ShapeDtypeStruct((R, D), bf),
        in_specs=[vmem] + ([vmem, vmem, hbm, hbm, smem] if fused else [vmem]) + [hbm, hbm],
        out_specs=vmem,
        scratch_shapes=extra
        + [
            pltpu.VMEM((C, nin, Kc), bf),
            pltpu.VMEM((4, N, Kc), f32),
            pltpu.VMEM((4, Z * R, Kc), f32),
            pltpu.VMEM((4, R, Kc), f32),
            pltpu.VMEM((C, N // 2, Kc), bf),
            pltpu.VMEM((C, N // 2, Kc), bf),
            pltpu.VMEM((C, Z * R, Kc), bf),
            pltpu.VMEM((C, Z * R, Kc), bf),
            pltpu.VMEM((C, Z * R, Kc), bf),
            pltpu.VMEM((C, Z - 1, R, Kc), bf),
            pltpu.SemaphoreType.DMA((C, Z - 1)),
            pltpu.SemaphoreType.DMA((C, Z - 1)),
            pltpu.SemaphoreType.DMA((C,)),
            pltpu.SemaphoreType.DMA((C,)),
            pltpu.SemaphoreType.DMA((C,)),
            pltpu.SemaphoreType.DMA((C,)),
            pltpu.SemaphoreType.DMA((C, 2)),
        ],
        compiler_params=pltpu.CompilerParams(
            collective_id=1, has_side_effects=True, vmem_limit_bytes=56 * MIB
        ),
        name="combine",
    )(x, *operands, wo, wd)


def block_scores(queries, key_block, lengths):
    scores = (
        jnp.einsum("rhd,rld->rhl", queries, key_block, preferred_element_type=jnp.float32) / 16.0
    )
    places = jnp.arange(key_block.shape[1], dtype=jnp.int32)
    live_mask = places[None, :] < lengths[:, None]
    return jnp.where(live_mask[:, None, :], scores, -1e30)


def attend_all(queries, new_key, new_value, cache_keys, cache_values, lengths):
    scores = block_scores(queries, cache_keys, lengths)
    own_score = (
        jnp.einsum("rhd,rd->rh", queries, new_key, preferred_element_type=jnp.float32) / 16.0
    )
    highest = jnp.maximum(jnp.max(scores, axis=2), own_score)
    weights = jnp.exp(scores - highest[:, :, None])
    own_weight = jnp.exp(own_score - highest)
    denominator = jnp.sum(weights, axis=2) + own_weight
    probs = (weights / denominator[:, :, None]).astype(jnp.bfloat16)
    own_prob = (own_weight / denominator).astype(jnp.bfloat16).astype(jnp.float32)
    attended = jnp.einsum("rhl,rld->rhd", probs, cache_values, preferred_element_type=jnp.float32)
    return attended + own_prob[:, :, None] * new_value.astype(jnp.float32)[:, None, :]


def shards(
    n,
    layer_input,
    norm_gain,
    w_query,
    w_keyval,
    w_out,
    w_gate,
    w_up,
    w_down,
    cache_keys,
    cache_values,
    lengths,
):
    R = layer_input.shape[0]
    Z = n // 4
    qkv, hidden = project(n, layer_input, norm_gain, w_query, w_keyval, w_gate, w_up)
    nq, nkv = w_query.shape[1], w_keyval.shape[1]
    if nq % 128 == 0 and w_out.shape[0] == nq:
        operands = (qkv, hidden, cache_keys, cache_values, lengths)
        return combine(n, layer_input, operands, w_out, w_down)
    query_cols = qkv[:, :nq]
    keyval_cols = qkv[:, qkv.shape[1] - 128 :][:, :nkv]

    def to_index_order(a):
        a = a.reshape(2, 2, Z, R, a.shape[1]).transpose(2, 1, 0, 3, 4)
        return a.reshape(n, R, a.shape[4])

    query_rows, keyval_rows = (
        lax.all_to_all(to_index_order(query_cols), "gx", split_axis=0, concat_axis=0, tiled=True),
        lax.all_to_all(to_index_order(keyval_cols), "gx", split_axis=0, concat_axis=0, tiled=True),
    )
    queries = query_rows.transpose(1, 0, 2).reshape(R, H, HD)
    keyval_rows = keyval_rows.transpose(1, 0, 2).reshape(R, 2 * HD)
    new_key = keyval_rows[:, :HD]
    new_value = keyval_rows[:, HD:]
    attended = attend_all(queries, new_key, new_value, cache_keys, cache_values, lengths)
    attended = attended.reshape(R, H * HD).astype(jnp.bfloat16)
    att = lax.all_to_all(
        attended.reshape(R, n, -1).transpose(1, 0, 2), "gx", split_axis=0, concat_axis=0, tiled=True
    )
    att = att.reshape(Z, 2, 2, R, -1).transpose(2, 1, 0, 3, 4).reshape(n * R, -1)
    lhs = jnp.concatenate([att, hidden], axis=1)
    return combine(n, layer_input, (lhs,), w_out, w_down)


def solution(mesh):
    n = mesh.shape["gx"]
    return jax.shard_map(
        functools.partial(shards, n),
        mesh=mesh,
        in_specs=(
            P(("grp", "gx"), None),
            P(),
            P(None, "gx"),
            P(None, "gx"),
            P("gx", None),
            P(None, "gx"),
            P(None, "gx"),
            P("gx", None),
            P(("grp", "gx"), None, None),
            P(("grp", "gx"), None, None),
            P(("grp", "gx")),
        ),
        out_specs=P(("grp", "gx"), None),
        check_vma=False,
    )
```

```python
import functools

import jax
import jax.numpy as jnp
from jax import lax
from jax.experimental import pallas as pl
from jax.experimental.pallas import tpu as pltpu
from jax.sharding import PartitionSpec as P

H = 24
HD = 256
MIB = 1024 * 1024


def places(Z):
    me = lax.axis_index("gx")
    z = lax.div(me, 4)
    y = lax.rem(lax.div(me, 2), 2)
    c = lax.rem(me, 2)
    return z, y, c


def index_of(z, y, c):
    return (z * 2 + y) * 2 + c


def partners(Z, z, y, c):
    out = [index_of(lax.rem(z + d, Z), y, c) for d in range(1, Z)]
    return out + [index_of(z, 1 - y, c), index_of(z, y, 1 - c)]


def greet(Z, z, y, c, everyone=False):
    barrier = pltpu.get_barrier_semaphore()
    me = index_of(z, y, c)
    if everyone:
        all_partners = [lax.rem(me + d, 4 * Z) for d in range(1, 4 * Z)]
    else:
        all_partners = partners(Z, z, y, c)
    for p in all_partners:
        pl.semaphore_signal(
            barrier, inc=1, device_id={"gx": p}, device_id_type=pl.DeviceIdType.MESH
        )
    return barrier


def remote(src, dst, send, recv, p):
    return pltpu.make_async_remote_copy(
        src_ref=src,
        dst_ref=dst,
        send_sem=send,
        recv_sem=recv,
        device_id={"gx": p},
        device_id_type=pl.DeviceIdType.MESH,
    )


def project_kernel(
    Z, R, C, Kc,
    x_ref, gain_ref, wq, wkv, wg, wu,
    qkv_out, hid_out,
    gbuf, wqb, wkvb, wgb, wub, accq, acckv, accg, accu,
    zsend, zrecv, ysend, yrecv, csend, crecv, wsem,
):
    z, y, c = places(Z)
    barrier = greet(Z, z, y, c)
    weights = ((wq, wqb), (wkv, wkvb), (wg, wgb), (wu, wub))
    AHEAD = 4
    LY, LC = 2, 1

    def wcopy(k, i):
        src, dst = weights[i]
        part = pl.ds(pl.multiple_of(k * Kc, Kc), Kc)
        src = src.at[part, :] if i == 0 else src.at[:, part]
        return pltpu.make_async_copy(src, dst.at[k], wsem.at[k, i])

    def wstart(k):
        for i in range(4):
            wcopy(k, i).start()

    for k in range(min(AHEAD, C)):
        wstart(k)

    D = C * Kc
    total = jnp.zeros((R, 1), jnp.float32)
    for k in range(C):
        total += jnp.sum(x_ref[:, k * Kc : (k + 1) * Kc].astype(jnp.float32), axis=1, keepdims=True)
    mean = total / D
    square = jnp.zeros((R, 1), jnp.float32)
    for k in range(C):
        centred = x_ref[:, k * Kc : (k + 1) * Kc].astype(jnp.float32) - mean
        square += jnp.sum(centred * centred, axis=1, keepdims=True)
    scale = lax.rsqrt(square / D + 1e-06)

    line = pl.multiple_of((c * 2 + y) * Z * R, R)
    other_line = pl.multiple_of((c * 2 + 1 - y) * Z * R, R)
    half = pl.multiple_of(c * 2 * Z * R, R)
    other_half = pl.multiple_of((1 - c) * 2 * Z * R, R)
    own = pl.multiple_of(((c * 2 + y) * Z + z) * R, R)
    for k in range(C):
        cols = slice(k * Kc, (k + 1) * Kc)
        centred = x_ref[:, cols].astype(jnp.float32) - mean
        gbuf[k, pl.ds(own, R), :] = (centred * scale * gain_ref[:, cols]).astype(jnp.bfloat16)

    def zcopy(k, d):
        ref = gbuf.at[k, pl.ds(own, R), :]
        return remote(
            ref, ref, zsend.at[k, d - 1], zrecv.at[k, d - 1], index_of(lax.rem(z + d, Z), y, c)
        )

    def zarrival(k, d):
        src = pl.multiple_of(((c * 2 + y) * Z + lax.rem(z + Z - d, Z)) * R, R)
        ref = gbuf.at[k, pl.ds(src, R), :]
        return remote(
            ref, ref, zsend.at[k, d - 1], zrecv.at[k, d - 1], index_of(lax.rem(z + d, Z), y, c)
        )

    def ycopy(k, base):
        ref = gbuf.at[k, pl.ds(base, Z * R), :]
        return remote(ref, ref, ysend.at[k], yrecv.at[k], index_of(z, 1 - y, c))

    def ccopy(k, base):
        ref = gbuf.at[k, pl.ds(base, 2 * Z * R), :]
        return remote(ref, ref, csend.at[k], crecv.at[k], index_of(z, y, 1 - c))

    accq[...] = jnp.zeros_like(accq)
    acckv[...] = jnp.zeros_like(acckv)
    accg[...] = jnp.zeros_like(accg)
    accu[...] = jnp.zeros_like(accu)

    pl.semaphore_wait(barrier, Z + 1)
    for k in range(min(2, C)):
        for d in range(1, Z):
            zcopy(k, d).start()

    def step(s, carry):
        @pl.when(s + AHEAD < C)
        def _():
            wstart(s + AHEAD)

        @pl.when(s + 2 < C)
        def _():
            for d in range(1, Z):
                zcopy(s + 2, d).start()

        @pl.when(s < C)
        def _():
            for d in range(1, Z):
                zarrival(s, d).wait_recv()
            ycopy(s, line).start()

        @pl.when(jnp.logical_and(s >= LY, s < C + LY))
        def _():
            k = s - LY
            ycopy(k, other_line).wait_recv()
            ccopy(k, half).start()

        @pl.when(s >= LY + LC)
        def _():
            k = s - LY - LC
            ccopy(k, other_half).wait_recv()
            for i in range(4):
                wcopy(k, i).wait()
            rows = gbuf[k]
            accq[...] += jnp.dot(rows, wqb[k], preferred_element_type=jnp.float32)
            for acc, w in ((acckv, wkvb), (accg, wgb), (accu, wub)):
                acc[...] += lax.dot_general(
                    rows, w[k], (((1,), (1,)), ((), ())), preferred_element_type=jnp.float32
                )

        return carry

    lax.fori_loop(0, C + LY + LC, step, 0)

    nq, nkv, wide = accq.shape[1], acckv.shape[1], qkv_out.shape[1]
    qkv_out[...] = jnp.zeros_like(qkv_out)
    qkv_out[:, 0:nq] = accq[...].astype(jnp.bfloat16)
    qkv_out[:, wide - 128 : wide - 128 + nkv] = acckv[...].astype(jnp.bfloat16)
    gate = accg[...]
    hid_out[...] = (gate * jax.nn.sigmoid(gate) * accu[...]).astype(jnp.bfloat16)

    def drain(k, carry):
        for d in range(1, Z):
            zcopy(k, d).wait_send()
        ycopy(k, line).wait_send()
        ccopy(k, half).wait_send()
        return carry

    lax.fori_loop(0, C, drain, 0)


def project(n, x, gain, wq, wkv, wg, wu):
    R, D = x.shape
    Z = n // 4
    Kc = 1024
    C = D // Kc
    N = n * R
    nq, nkv, ng = wq.shape[1], wkv.shape[1], wg.shape[1]
    vmem = pl.BlockSpec(memory_space=pltpu.VMEM)
    hbm = pl.BlockSpec(memory_space=pl.ANY)
    bf, f32 = jnp.bfloat16, jnp.float32
    return pl.pallas_call(
        functools.partial(project_kernel, Z, R, C, Kc),
        out_shape=[
            jax.ShapeDtypeStruct((N, -(-nq // 128) * 128 + 128), bf),
            jax.ShapeDtypeStruct((N, ng), bf),
        ],
        in_specs=[vmem, vmem, hbm, hbm, hbm, hbm],
        out_specs=[vmem, vmem],
        scratch_shapes=[
            pltpu.VMEM((C, N, Kc), bf),
            pltpu.VMEM((C, Kc, nq), bf),
            pltpu.VMEM((C, nkv, Kc), bf),
            pltpu.VMEM((C, ng, Kc), bf),
            pltpu.VMEM((C, ng, Kc), bf),
            pltpu.VMEM((N, nq), f32),
            pltpu.VMEM((N, nkv), f32),
            pltpu.VMEM((N, ng), f32),
            pltpu.VMEM((N, ng), f32),
            pltpu.SemaphoreType.DMA((C, Z - 1)),
            pltpu.SemaphoreType.DMA((C, Z - 1)),
            pltpu.SemaphoreType.DMA((C,)),
            pltpu.SemaphoreType.DMA((C,)),
            pltpu.SemaphoreType.DMA((C,)),
            pltpu.SemaphoreType.DMA((C,)),
            pltpu.SemaphoreType.DMA((C, 4)),
        ],
        compiler_params=pltpu.CompilerParams(
            collective_id=0, has_side_effects=True, vmem_limit_bytes=56 * MIB
        ),
        name="project",
    )(x, gain.reshape(1, D), wq, wkv.T, wg.T, wu.T)


def attend(
    Z, R, z, y, c,
    qkv_ref, keys, values, len_ref, lhs_ref,
    qrecv, qall, score, prob, att, asend, keyb, valb,
    q_send, q_recv, a_send, a_recv, kv_sem,
    barrier,
):
    n = 4 * Z
    me = index_of(z, y, c)
    L = keyb.shape[1]
    nq = asend.shape[2]
    nkv = 2 * HD // n
    per = nq // 128
    M = H * R
    bf, f32 = jnp.bfloat16, jnp.float32
    kcopy = pltpu.make_async_copy(keys, keyb, kv_sem.at[0])
    vcopy = pltpu.make_async_copy(values, valb, kv_sem.at[1])
    kcopy.start()
    vcopy.start()

    def row_of(p):
        place = (lax.rem(p, 2) * 2 + lax.rem(lax.div(p, 2), 2)) * Z + lax.div(p, 4)
        return pl.multiple_of(place * R, R)

    def qcopy(d):
        to = lax.rem(me + d, n)
        return remote(
            qkv_ref.at[pl.ds(row_of(to), R), :], qrecv.at[me], q_send.at[d], q_recv.at[d], to
        )

    def qarrival(d):
        source = lax.rem(me + n - d, n)
        return remote(
            qkv_ref.at[pl.ds(row_of(me), R), :],
            qrecv.at[source],
            q_send.at[d],
            q_recv.at[d],
            lax.rem(me + d, n),
        )

    def acopy(d):
        to = lax.rem(me + d, n)
        return remote(
            asend.at[to],
            lhs_ref.at[pl.ds(row_of(me), R), pl.ds(0, nq)],
            a_send.at[d],
            a_recv.at[d],
            to,
        )

    def aarrival(d):
        source = lax.rem(me + n - d, n)
        return remote(
            asend.at[me],
            lhs_ref.at[pl.ds(row_of(source), R), pl.ds(0, nq)],
            a_send.at[d],
            a_recv.at[d],
            lax.rem(me + d, n),
        )

    def each(f):
        for d in sorted(range(1, n), key=lambda d: abs(n - 2 * d)):
            f(d)

    pl.semaphore_wait(barrier, n - 1)
    each(lambda d: qcopy(d).start())
    qrecv[me] = qkv_ref[pl.ds(row_of(me), R), :]
    each(lambda d: qarrival(d).wait_recv())

    for b in range(2 * H):
        qall[(b // 2) * R : (b // 2 + 1) * R, (b % 2) * 128 : (b % 2 + 1) * 128] = qrecv[
            b // per, :, (b % per) * 128 : (b % per + 1) * 128
        ]
    wide = qrecv.shape[2]
    pieces = [qrecv[p, :, wide - 128 :].astype(f32)[:, :nkv] for p in range(n)]
    new_key = jnp.concatenate(pieces[: n // 2], axis=1)
    new_value = jnp.concatenate(pieces[n // 2 :], axis=1)

    row_in_head = lax.rem(lax.broadcasted_iota(jnp.int32, (M, L), 0), R)
    kcopy.wait()

    def score_rows(i, carry):
        picked = score[...]
        for j in range(8):
            r = i * 8 + j
            s = lax.dot_general(
                qall[...], keyb[r], (((1,), (1,)), ((), ())), preferred_element_type=f32
            )
            picked = jnp.where(row_in_head == r, s, picked)
        score[...] = picked
        return carry

    score[...] = jnp.zeros_like(score)
    lax.fori_loop(0, R // 8, score_rows, 0)

    row = lax.broadcasted_iota(jnp.int32, (R, L), 0)
    length = jnp.zeros((R, L), jnp.int32)
    for r in range(R):
        length = jnp.where(row == r, len_ref[r], length)
    live = lax.broadcasted_iota(jnp.int32, (R, L), 1) < length
    for h in range(H):
        rows = slice(h * R, (h + 1) * R)
        s = jnp.where(live, score[rows, :] / 16.0, -1e30)
        own = jnp.sum(qall[rows, :].astype(f32) * new_key, axis=1, keepdims=True) / 16.0
        highest = jnp.maximum(jnp.max(s, axis=1, keepdims=True), own)
        weights = jnp.exp(s - highest)
        own_weight = jnp.exp(own - highest)
        denominator = jnp.sum(weights, axis=1, keepdims=True) + own_weight
        prob[rows, :] = (weights / denominator).astype(bf).astype(f32)
        own_prob = (own_weight / denominator).astype(bf).astype(f32)
        att[rows, :] = own_prob * new_value

    vcopy.wait()

    def value_rows(i, carry):
        total = att[...]
        for j in range(8):
            r = i * 8 + j
            p = jnp.where(row_in_head == r, prob[...], 0.0).astype(bf)
            total = total + jnp.dot(p, valb[r], preferred_element_type=f32)
        att[...] = total
        return carry

    lax.fori_loop(0, R // 8, value_rows, 0)

    for b in range(2 * H):
        asend[b // per, :, (b % per) * 128 : (b % per + 1) * 128] = att[
            (b // 2) * R : (b // 2 + 1) * R, (b % 2) * 128 : (b % 2 + 1) * 128
        ].astype(bf)
    each(lambda d: acopy(d).start())
    lhs_ref[pl.ds(row_of(me), R), pl.ds(0, nq)] = asend[me]
    each(lambda d: aarrival(d).wait_recv())

    def drain():
        each(lambda d: qcopy(d).wait_send())
        each(lambda d: acopy(d).wait_send())

    return drain


def combine_kernel(
    Z, R, C, Kc, fused,
    x_ref, *refs,
):
    if fused:
        qkv_ref, hid_ref, keys, values, len_ref, wo, wd, out_ref, lhs_ref = refs[:9]
        attend_scratch = refs[9:22]
        refs = refs[22:]
    else:
        lhs_ref, wo, wd, out_ref = refs[:4]
        refs = refs[4:]
    (
        wbuf, part, lineb, ownb, csb, crb, ysb, yrb, zsb, zrb,
        zsend, zrecv, ysend, yrecv, csend, crecv, wsem,
    ) = refs
    z, y, c = places(Z)
    barrier = greet(Z, z, y, c, fused)
    no, nd = wo.shape[0], wd.shape[0]
    AHEAD = 4
    LC, LY, LZ = 1, 2, 2

    def wcopies(k):
        cols = pl.ds(pl.multiple_of(k * Kc, Kc), Kc)
        return (
            pltpu.make_async_copy(wo.at[:, cols], wbuf.at[k, pl.ds(0, no), :], wsem.at[k, 0]),
            pltpu.make_async_copy(wd.at[:, cols], wbuf.at[k, pl.ds(no, nd), :], wsem.at[k, 1]),
        )

    def wstart(k):
        for copy in wcopies(k):
            copy.start()

    for k in range(min(AHEAD, C)):
        wstart(k)

    half = pl.multiple_of(c * 2 * Z * R, R)
    other_half = pl.multiple_of((1 - c) * 2 * Z * R, R)
    line = pl.multiple_of(y * Z * R, R)
    other_line = pl.multiple_of((1 - y) * Z * R, R)
    own = pl.multiple_of(z * R, R)

    def ccopy(k):
        return remote(csb.at[k], crb.at[k], csend.at[k], crecv.at[k], index_of(z, y, 1 - c))

    def ycopy(k):
        return remote(ysb.at[k], yrb.at[k], ysend.at[k], yrecv.at[k], index_of(z, 1 - y, c))

    def zcopy(k, d):
        to = lax.rem(z + d, Z)
        return remote(
            zsb.at[k, pl.ds(pl.multiple_of(to * R, R), R), :],
            zrb.at[k, d - 1],
            zsend.at[k, d - 1],
            zrecv.at[k, d - 1],
            index_of(to, y, c),
        )

    if fused:
        lhs_ref[:, no:] = hid_ref[...]
        finish = attend(
            Z, R, z, y, c, qkv_ref, keys, values, len_ref, lhs_ref, *attend_scratch, barrier
        )
    else:
        pl.semaphore_wait(barrier, Z + 1)

    def step(s, carry):
        @pl.when(s + AHEAD < C)
        def _():
            wstart(s + AHEAD)

        @pl.when(s < C)
        def _():
            for copy in wcopies(s):
                copy.wait()
            slot = lax.rem(s, 4)
            part[slot] = jnp.dot(lhs_ref[...], wbuf[s], preferred_element_type=jnp.float32)
            csb[s] = part[slot, pl.ds(other_half, 2 * Z * R), :].astype(jnp.bfloat16)
            ccopy(s).start()

        @pl.when(jnp.logical_and(s >= LC, s < C + LC))
        def _():
            k = s - LC
            slot = lax.rem(k, 4)
            ccopy(k).wait_recv()
            ysb[k] = (
                part[slot, pl.ds(half + other_line, Z * R), :]
                + crb[k, pl.ds(other_line, Z * R), :].astype(jnp.float32)
            ).astype(jnp.bfloat16)
            ycopy(k).start()
            lineb[slot] = part[slot, pl.ds(half + line, Z * R), :] + crb[
                k, pl.ds(line, Z * R), :
            ].astype(jnp.float32)

        @pl.when(jnp.logical_and(s >= LC + LY, s < C + LC + LY))
        def _():
            k = s - LC - LY
            slot = lax.rem(k, 4)
            ycopy(k).wait_recv()
            lineb[slot] = lineb[slot] + yrb[k].astype(jnp.float32)
            zsb[k] = lineb[slot].astype(jnp.bfloat16)
            for d in range(1, Z):
                zcopy(k, d).start()
            ownb[slot] = lineb[slot, pl.ds(own, R), :]

        @pl.when(s >= LC + LY + LZ)
        def _():
            k = s - LC - LY - LZ
            slot = lax.rem(k, 4)
            cols = pl.ds(pl.multiple_of(k * Kc, Kc), Kc)
            total = ownb[slot]
            for d in range(1, Z):
                zcopy(k, d).wait_recv()
                total = total + zrb[k, d - 1].astype(jnp.float32)
            out_ref[:, cols] = (x_ref[:, cols].astype(jnp.float32) + total).astype(jnp.bfloat16)

        return carry

    lax.fori_loop(0, C + LC + LY + LZ, step, 0)

    def drain(k, carry):
        for d in range(1, Z):
            zcopy(k, d).wait_send()
        ycopy(k).wait_send()
        ccopy(k).wait_send()
        return carry

    lax.fori_loop(0, C, drain, 0)
    if fused:
        finish()


def combine(n, x, operands, wo, wd):
    fused = len(operands) > 1
    R, D = x.shape
    Z = n // 4
    Kc = 1024
    C = D // Kc
    N = n * R
    vmem = pl.BlockSpec(memory_space=pltpu.VMEM)
    hbm = pl.BlockSpec(memory_space=pl.ANY)
    smem = pl.BlockSpec(memory_space=pltpu.SMEM)
    bf, f32 = jnp.bfloat16, jnp.float32
    nq, nin = wo.shape[0], wo.shape[0] + wd.shape[0]
    extra = []
    if fused:
        qkv, _, keys, _, _ = operands
        L = keys.shape[1]
        extra = [
            pltpu.VMEM((N, nin), bf),
            pltpu.VMEM((n, R, qkv.shape[1]), bf),
            pltpu.VMEM((H * R, HD), bf),
            pltpu.VMEM((H * R, L), f32),
            pltpu.VMEM((H * R, L), f32),
            pltpu.VMEM((H * R, HD), f32),
            pltpu.VMEM((n, R, nq), bf),
            pltpu.VMEM((R, L, HD), bf),
            pltpu.VMEM((R, L, HD), bf),
            pltpu.SemaphoreType.DMA((n,)),
            pltpu.SemaphoreType.DMA((n,)),
            pltpu.SemaphoreType.DMA((n,)),
            pltpu.SemaphoreType.DMA((n,)),
            pltpu.SemaphoreType.DMA((2,)),
        ]
    return pl.pallas_call(
        functools.partial(combine_kernel, Z, R, C, Kc, fused),
        out_shape=jax.ShapeDtypeStruct((R, D), bf),
        in_specs=[vmem] + ([vmem, vmem, hbm, hbm, smem] if fused else [vmem]) + [hbm, hbm],
        out_specs=vmem,
        scratch_shapes=extra
        + [
            pltpu.VMEM((C, nin, Kc), bf),
            pltpu.VMEM((4, N, Kc), f32),
            pltpu.VMEM((4, Z * R, Kc), f32),
            pltpu.VMEM((4, R, Kc), f32),
            pltpu.VMEM((C, N // 2, Kc), bf),
            pltpu.VMEM((C, N // 2, Kc), bf),
            pltpu.VMEM((C, Z * R, Kc), bf),
            pltpu.VMEM((C, Z * R, Kc), bf),
            pltpu.VMEM((C, Z * R, Kc), bf),
            pltpu.VMEM((C, Z - 1, R, Kc), bf),
            pltpu.SemaphoreType.DMA((C, Z - 1)),
            pltpu.SemaphoreType.DMA((C, Z - 1)),
            pltpu.SemaphoreType.DMA((C,)),
            pltpu.SemaphoreType.DMA((C,)),
            pltpu.SemaphoreType.DMA((C,)),
            pltpu.SemaphoreType.DMA((C,)),
            pltpu.SemaphoreType.DMA((C, 2)),
        ],
        compiler_params=pltpu.CompilerParams(
            collective_id=1, has_side_effects=True, vmem_limit_bytes=56 * MIB
        ),
        name="combine",
    )(x, *operands, wo, wd)


def block_scores(queries, key_block, lengths):
    scores = (
        jnp.einsum("rhd,rld->rhl", queries, key_block, preferred_element_type=jnp.float32) / 16.0
    )
    places = jnp.arange(key_block.shape[1], dtype=jnp.int32)
    live_mask = places[None, :] < lengths[:, None]
    return jnp.where(live_mask[:, None, :], scores, -1e30)


def attend_all(queries, new_key, new_value, cache_keys, cache_values, lengths):
    scores = block_scores(queries, cache_keys, lengths)
    own_score = (
        jnp.einsum("rhd,rd->rh", queries, new_key, preferred_element_type=jnp.float32) / 16.0
    )
    highest = jnp.maximum(jnp.max(scores, axis=2), own_score)
    weights = jnp.exp(scores - highest[:, :, None])
    own_weight = jnp.exp(own_score - highest)
    denominator = jnp.sum(weights, axis=2) + own_weight
    probs = (weights / denominator[:, :, None]).astype(jnp.bfloat16)
    own_prob = (own_weight / denominator).astype(jnp.bfloat16).astype(jnp.float32)
    attended = jnp.einsum("rhl,rld->rhd", probs, cache_values, preferred_element_type=jnp.float32)
    return attended + own_prob[:, :, None] * new_value.astype(jnp.float32)[:, None, :]


def shards(
    n,
    layer_input,
    norm_gain,
    w_query,
    w_keyval,
    w_out,
    w_gate,
    w_up,
    w_down,
    cache_keys,
    cache_values,
    lengths,
):
    R = layer_input.shape[0]
    Z = n // 4
    qkv, hidden = project(n, layer_input, norm_gain, w_query, w_keyval, w_gate, w_up)
    nq, nkv = w_query.shape[1], w_keyval.shape[1]
    if nq % 128 == 0 and w_out.shape[0] == nq:
        operands = (qkv, hidden, cache_keys, cache_values, lengths)
        return combine(n, layer_input, operands, w_out, w_down)
    query_cols = qkv[:, :nq]
    keyval_cols = qkv[:, qkv.shape[1] - 128 :][:, :nkv]

    def to_index_order(a):
        a = a.reshape(2, 2, Z, R, a.shape[1]).transpose(2, 1, 0, 3, 4)
        return a.reshape(n, R, a.shape[4])

    query_rows, keyval_rows = (
        lax.all_to_all(to_index_order(query_cols), "gx", split_axis=0, concat_axis=0, tiled=True),
        lax.all_to_all(to_index_order(keyval_cols), "gx", split_axis=0, concat_axis=0, tiled=True),
    )
    queries = query_rows.transpose(1, 0, 2).reshape(R, H, HD)
    keyval_rows = keyval_rows.transpose(1, 0, 2).reshape(R, 2 * HD)
    new_key = keyval_rows[:, :HD]
    new_value = keyval_rows[:, HD:]
    attended = attend_all(queries, new_key, new_value, cache_keys, cache_values, lengths)
    attended = attended.reshape(R, H * HD).astype(jnp.bfloat16)
    att = lax.all_to_all(
        attended.reshape(R, n, -1).transpose(1, 0, 2), "gx", split_axis=0, concat_axis=0, tiled=True
    )
    att = att.reshape(Z, 2, 2, R, -1).transpose(2, 1, 0, 3, 4).reshape(n * R, -1)
    lhs = jnp.concatenate([att, hidden], axis=1)
    return combine(n, layer_input, (lhs,), w_out, w_down)


def solution(mesh):
    n = mesh.shape["gx"]
    return jax.shard_map(
        functools.partial(shards, n),
        mesh=mesh,
        in_specs=(
            P(("grp", "gx"), None),
            P(),
            P(None, "gx"),
            P(None, "gx"),
            P("gx", None),
            P(None, "gx"),
            P(None, "gx"),
            P("gx", None),
            P(("grp", "gx"), None, None),
            P(("grp", "gx"), None, None),
            P(("grp", "gx")),
        ),
        out_specs=P(("grp", "gx"), None),
        check_vma=False,
    )
```
